32 devices in a mesh: grp: 8 (over z, x), rep: 4 (over y, core).
Axes of the slice: x: 2, y: 2, z: 4, core: 2. Of those that a mesh axis runs over, the one named last changes fastest.
Arguments:
- embeddings: bfloat16 [8192, 1024], P(('grp', 'rep')), may hold values from -15 to 15
- scales: float32 [8192, 8], P(('grp', 'rep')), may hold values from 0.05 to 0.5
- cluster: int32 [8192], P(('grp', 'rep')), may hold values from 0 to 95, as said below
- cluster_rank: int32 [8192], P(('grp', 'rep')), may hold values from 0 to 63, as said below
Outputs:
- best_cosine: float32 [8192], P(('grp', 'rep'))
The draws below stay inside these ranges and needn't reach their ends.
Inputs may be any that keep to these rules, and one draw needn't show every extreme that they name: cluster // 12 names the owner of a row's cluster among 8 and cluster % 12 its place there; clusters of different shards are different even with equal numbers. Among the rows of one device at most 96 have the same owner, and in every draw some owner is named by exactly 96 rows of every device of its shard. `cluster_rank`: within one cluster the ranks of its rows are 0 to its size minus 1, each once; a cluster holds at most 64 rows, and in every draw some cluster holds exactly 64.
All inputs are finite; a program needn't handle non-finite values.
Results may differ from the reference program's by a relative error of at most 0.00035.
The reference program's roundings to bfloat16 on the way (of `values`, `inverse_root` and `whitened`) count: a program that leaves them out, or rounds other values in their place, can miss the bound.
Values may be sent and summed in bfloat16 or wider, within the bound.
No kernel may reach another device: no remote copies, remote signals or barrier semaphores. Data moves between devices by JAX's collectives and lax.ppermute only.
A program may use at most 64 MiB of HBM per device.

```python
import math
import jax
import jax.numpy as jnp
from jax import lax

D = 1024
BLK = 128
ROWS_DEV = 256
CMAX = 64
STEPS = 5
SLOT = 96
CPO = 12
CLUSTERS = 96
ROWS_ALL = 8192
N_GRP = 8
N_REP = 4


def shard_layout(shard_key):
    order_key, count_key, source_key, cell_key = jax.random.split(shard_key, 4)
    owner_rank = jax.random.permutation(order_key, N_GRP).astype(jnp.int32)
    remaining = ROWS_DEV - SLOT
    base_count = remaining // (N_GRP - 1)
    leftover = remaining - base_count * (N_GRP - 1)
    half_base = base_count // 2
    pair_total = (N_GRP - 1) // 2

    def source_counts(one_key):
        perm_key, swap_key = jax.random.split(one_key)
        ranking = jax.random.permutation(perm_key, N_GRP - 1)
        counts = base_count + (ranking < leftover).astype(jnp.int32)
        swap_size = jax.random.randint(swap_key, (pair_total,), -half_base, half_base + 1).astype(jnp.int32)
        change = jnp.zeros((N_GRP - 1,), jnp.int32)
        change = change.at[0:2 * pair_total:2].add(swap_size).at[1:2 * pair_total:2].add(-swap_size)
        return jnp.concatenate([jnp.full((1,), SLOT, jnp.int32), counts + change])
    by_rank = jax.vmap(source_counts)(jax.random.split(count_key, N_GRP))
    by_owner = by_rank[:, owner_rank]
    seg_ends = jnp.cumsum(by_owner, axis=1)
    seg_starts = seg_ends - by_owner

    def source_rows(one_key, src_ends, src_starts):
        position = jax.random.permutation(one_key, ROWS_DEV).astype(jnp.int32)
        owner_of = jnp.sum((src_ends[None, :] <= position[:, None]).astype(jnp.int32), axis=1)
        return (owner_of, position - src_starts[owner_of])
    owner_of, within = jax.vmap(source_rows)(jax.random.split(source_key, N_GRP), seg_ends, seg_starts)
    cell_total = N_GRP * SLOT

    def owner_cells(one_key, counts_in):
        shuffle = jax.random.permutation(one_key, cell_total).astype(jnp.int32)
        filled = (jnp.arange(SLOT)[None, :] < counts_in[:, None]).reshape(cell_total).astype(jnp.int32)
        occupied = jnp.zeros((cell_total,), jnp.int32).at[shuffle].set(filled)
        cell_grid = occupied.reshape(CPO, CMAX)
        earlier = jnp.cumsum(cell_grid, axis=1) - cell_grid
        return (shuffle, earlier.reshape(cell_total))
    shuffle, earlier = jax.vmap(owner_cells)(jax.random.split(cell_key, N_GRP), by_owner.T)
    source = jnp.arange(N_GRP, dtype=jnp.int32)[:, None]
    slot_pos = source * SLOT + within
    cell_of = shuffle[owner_of, slot_pos]
    cluster = owner_of * CPO + cell_of // CMAX
    rank_of = earlier[owner_of, cell_of]
    return (cluster, rank_of)


def layout(key):
    base_key = jax.random.fold_in(key, 4711)
    cluster, rank_of = jax.vmap(shard_layout)(jax.random.split(base_key, N_REP))
    cluster = jnp.transpose(cluster, (1, 0, 2)).reshape(ROWS_ALL).astype(jnp.int32)
    rank_of = jnp.transpose(rank_of, (1, 0, 2)).reshape(ROWS_ALL).astype(jnp.int32)
    return (cluster, rank_of)


def draw_cluster(key, part):
    return layout(key)[0]


def draw_cluster_rank(key, part):
    return layout(key)[1]


def draw_embeddings(key, part):
    cluster = layout(key)[0]
    base_key = jax.random.fold_in(key, 9127)
    key_list = jax.random.split(base_key, 6)
    row_ids = jnp.arange(ROWS_ALL)
    device_block = row_ids // ROWS_DEV
    shard_of = device_block % N_REP
    centroid = jax.random.normal(key_list[0], (N_REP * CLUSTERS, D), jnp.float32)
    picked = centroid[shard_of * CLUSTERS + cluster]
    jitter = jax.random.normal(key_list[1], (ROWS_ALL, D), jnp.float32)
    spread = jnp.exp(jax.random.uniform(key_list[2], (D,), jnp.float32, jnp.log(0.2), jnp.log(2.0)))
    block_total = ROWS_ALL // ROWS_DEV
    device_lean = jax.random.normal(key_list[3], (block_total, D), jnp.float32) * (12.0 / jnp.sqrt(D * 1.0))
    row_tilt = jax.random.normal(key_list[4], (ROWS_ALL, 1), jnp.float32)
    offset = 0.8 * jax.random.normal(key_list[5], (D,), jnp.float32)
    rising = 1.0 + 2.0 * device_block.astype(jnp.float32) / (block_total - 1)
    values = rising[:, None] * (spread[None, :] * (jitter + 1.2 * picked) + offset[None, :] + row_tilt * device_lean[device_block])
    return jnp.clip(0.4 * values, -15.0, 15.0).astype(jnp.bfloat16)


def level_of(rng, shape, cuts, low, largest):
    level = 1.0
    for dim, blocks in cuts:
        draws = jax.random.uniform(jax.random.fold_in(jax.random.fold_in(rng, 6), dim), (blocks,), jnp.float32, low / len(cuts), largest / len(cuts))
        level = level * jnp.repeat(jnp.exp(draws), shape[dim] // blocks).reshape((-1,) + (1,) * (len(shape) - 1 - dim))
    return level


def setup_inputs(seed: int = 0) -> dict:
    keys = jax.random.split(jax.random.key(seed), 5)
    return {
        "embeddings": draw_embeddings(jax.random.fold_in(keys[4], 71), 0),
        "scales": jnp.clip(jnp.exp(math.log(0.5) - 2.3025851 * jax.random.uniform(keys[1], (ROWS_ALL, D // BLK), jnp.float32) ** level_of(keys[1], (ROWS_ALL, D // BLK), ((0, 32),), -0.2, 0.2)), 0.05, 0.5),
        "cluster": draw_cluster(jax.random.fold_in(keys[4], 71), 0),
        "cluster_rank": draw_cluster_rank(jax.random.fold_in(keys[4], 71), 0),
    }


COV_EPS = 0.001
UNIT_EPS = 1e-06
EXACT_MODE = lax.Precision.HIGHEST

def whiten(values, inverse_root, average):
    offset = jnp.dot(average[None, :], inverse_root.astype(jnp.float32), precision=EXACT_MODE)
    projected = jnp.dot(values, inverse_root, preferred_element_type=jnp.float32) - offset
    energy = lax.optimization_barrier(jnp.sum(projected * projected, axis=1, keepdims=True))
    return (projected * lax.rsqrt(energy + UNIT_EPS)).astype(jnp.bfloat16)

def best_within(table, occupied, cluster_count):
    feat_dim = table.shape[1]
    tile_rows = table.astype(jnp.float32).reshape(cluster_count, CMAX, feat_dim)
    similar = jnp.einsum('cmd,cnd->cmn', tile_rows, tile_rows, precision=EXACT_MODE)
    present = occupied.reshape(cluster_count, CMAX)
    distinct = lax.broadcasted_iota(jnp.int32, (1, CMAX, CMAX), 1) != lax.broadcasted_iota(jnp.int32, (1, CMAX, CMAX), 2)
    allowed = present[:, :, None] & present[:, None, :] & distinct
    highest = lax.optimization_barrier(jnp.max(jnp.where(allowed, similar, -jnp.inf), axis=2))
    return jnp.maximum(highest, -1.0).reshape(cluster_count * CMAX)

def reference(embeddings, scales, cluster, cluster_rank):
    row_total, feat_dim = embeddings.shape
    num_blocks = scales.shape[1]
    grouped = embeddings.astype(jnp.float32).reshape(row_total, num_blocks, feat_dim // num_blocks) * scales[:, :, None]
    values = grouped.reshape(row_total, feat_dim).astype(jnp.bfloat16)
    gram_sum = lax.dot_general(values, values, (((0,), (0,)), ((), ())), preferred_element_type=jnp.float32)
    column_total = lax.optimization_barrier(jnp.sum(values, axis=0, dtype=jnp.float32))
    average = column_total / row_total
    identity = jnp.eye(feat_dim, dtype=jnp.float32)
    centred = gram_sum / row_total - average[:, None] * average[None, :] + COV_EPS * identity
    normed = centred / jnp.sqrt(jnp.sum(centred * centred))
    current = identity
    for repeat in range(STEPS):
        product = jnp.dot(normed, current, precision=EXACT_MODE)
        product = jnp.dot(product, current, precision=EXACT_MODE)
        product = jnp.dot(product, current, precision=EXACT_MODE)
        current = 1.5 * current - 0.5 * product
    inverse_root = current.astype(jnp.bfloat16)
    whitened = whiten(values, inverse_root, average)
    per_device = row_total // (N_GRP * N_REP)
    shard_units = whitened.reshape(N_GRP, N_REP, per_device, feat_dim).transpose(1, 0, 2, 3).reshape(N_REP, N_GRP * per_device, feat_dim)
    cell_all = (cluster * CMAX + cluster_rank).astype(jnp.int32)
    shard_cells = cell_all.reshape(N_GRP, N_REP, per_device).transpose(1, 0, 2).reshape(N_REP, N_GRP * per_device)
    cell_count = CLUSTERS * CMAX

    def one_shard(pair_in):
        unit_rows, cell_index = pair_in
        table = jnp.zeros((cell_count, feat_dim), jnp.bfloat16).at[cell_index].set(unit_rows)
        occupied = jnp.zeros((cell_count,), jnp.int32).at[cell_index].set(1) > 0
        return best_within(table, occupied, CLUSTERS)[cell_index]
    result = lax.map(one_shard, (shard_units, shard_cells))
    return result.reshape(N_REP, N_GRP, per_device).transpose(1, 0, 2).reshape(row_total)
```

```python
import functools

import jax
import jax.numpy as jnp
from jax import lax
from jax.experimental import pallas as pl
from jax.experimental.pallas import tpu as pltpu
from jax.sharding import PartitionSpec as P

STEPS = 5
COV_EPS = 0.001
UNIT_EPS = 1e-06
EDGE = 128
F32 = jnp.float32
BF16 = jnp.bfloat16
VMEM_BYTES = 50 * 2**20


def swap(array, axis, bit):
    size = lax.axis_size(axis)
    return lax.ppermute(array, axis, [(i, i ^ bit) for i in range(size)])


def whole(count):
    return [pl.BlockSpec(memory_space=pltpu.VMEM)] * count


def call(kernel, outs, ins, flops=0, scratch=()):
    moved = sum(a.size * a.dtype.itemsize for a in list(ins) + list(outs))
    return pl.pallas_call(
        kernel,
        out_shape=outs,
        in_specs=whole(len(ins)),
        out_specs=whole(len(outs)),
        scratch_shapes=list(scratch),
        compiler_params=pltpu.CompilerParams(vmem_limit_bytes=VMEM_BYTES),
        cost_estimate=pl.CostEstimate(flops=flops, bytes_accessed=moved, transcendentals=0),
    )(*ins)


def shape(rows, columns, dtype=F32):
    return jax.ShapeDtypeStruct((rows, columns), dtype)


def core_bit():
    return lax.axis_index("rep") % 2


def y_bit():
    return lax.axis_index("rep") // 2


def x_bit():
    return lax.axis_index("grp") % 2


def z_pos():
    return lax.axis_index("grp") // 2


def block_rows(blocks):
    total = blocks * (blocks + 1) // 2
    halves, room = ([], []), total // 2
    for i in range(blocks):
        if blocks - i <= room:
            halves[0].append(i)
            room -= blocks - i
        else:
            halves[1].append(i)
    return halves


def packed_places(blocks):
    places = []
    for rows in block_rows(blocks):
        pairs = [(i, j) for i in rows for j in range(i, blocks)]
        places.append([(i, j, EDGE * k) for k, (i, j) in enumerate(pairs)])
    return places


def dequantize_kernel(emb_ref, scale_ref, out_ref):
    blocks = scale_ref.shape[1]
    width = emb_ref.shape[1] // blocks
    for b in range(blocks):
        columns = pl.ds(b * width, width)
        out_ref[:, columns] = (
            emb_ref[:, columns].astype(F32) * scale_ref[:, b : b + 1]
        ).astype(BF16)


def gram_kernel(own_ref, other_ref, a_keep, a_send, b_keep, b_send, packed):
    blocks = own_ref.shape[1] // EDGE
    contract = (((0,), (0,)), ((), ()))
    core, x, y = core_bit(), x_bit(), y_bit()
    row = lax.broadcasted_iota(jnp.int32, (EDGE, EDGE), 0)
    column = lax.broadcasted_iota(jnp.int32, (EDGE, EDGE), 1)
    half = EDGE // 2
    places = packed_places(blocks)
    if packed.shape[0] > EDGE * len(places[0]):
        packed[...] = jnp.zeros_like(packed)
    for side in range(2):

        @pl.when(core == side)
        def _():
            first = {(i, j): start for i, j, start in places[side]}
            for i in block_rows(blocks)[side]:
                mine = pl.ds(i * EDGE, EDGE)
                rest = pl.ds(i * EDGE, (blocks - i) * EDGE)
                total = lax.dot_general(
                    own_ref[:, mine], own_ref[:, rest], contract, preferred_element_type=F32
                ) + lax.dot_general(
                    other_ref[:, mine], other_ref[:, rest], contract, preferred_element_type=F32
                )
                sums = jnp.sum(own_ref[:, mine].astype(F32), axis=0, keepdims=True) + jnp.sum(
                    other_ref[:, mine].astype(F32), axis=0, keepdims=True
                )
                turned = pltpu.roll(jnp.broadcast_to(sums, (8, EDGE)), half, 1)[0:1]
                diagonal = total[:, :EDGE]
                diagonal = jnp.where((row == EDGE - 1) & (column < half), sums, diagonal)
                diagonal = jnp.where((row == EDGE - 2) & (column < half), turned, diagonal)
                packed[pl.ds(first[i, i], EDGE), :] = diagonal
                for j in range(i + 1, blocks):
                    packed[pl.ds(first[i, j], EDGE), :] = total[
                        :, (j - i) * EDGE : (j - i + 1) * EDGE
                    ]

    part = a_keep.shape[0]
    a_keep[...] = packed[pl.ds(x * part, part), :]
    a_send[...] = packed[pl.ds((1 - x) * part, part), :]
    b_keep[...] = packed[pl.ds((2 + y) * part, part), :]
    b_send[...] = packed[pl.ds((3 - y) * part, part), :]


def halve_kernel(which, keep_ref, got_ref, keep_out, send_out):
    bit = which()
    part = keep_out.shape[0]
    mine, theirs = pl.ds(bit * part, part), pl.ds((1 - bit) * part, part)
    keep_out[...] = keep_ref[mine, :] + got_ref[mine, :]
    send_out[...] = keep_ref[theirs, :] + got_ref[theirs, :]


def line_split_kernel(length, a_keep, a_got, b_keep, b_got, *outs):
    z = z_pos()
    part = a_keep.shape[0] // length
    for d in range(length):
        rows = pl.ds((z ^ d) * part, part)
        outs[d][:part, :] = a_keep[rows, :] + a_got[rows, :]
        outs[d][part:, :] = b_keep[rows, :] + b_got[rows, :]


def line_sum_kernel(*refs):
    total = refs[0][...]
    for ref in refs[1:-1]:
        total = total + ref[...]
    refs[-1][...] = total


def line_join_kernel(length, *refs):
    z = z_pos()
    a_out, b_out = refs[-2:]
    part = a_out.shape[0] // length
    for d in range(length):
        rows = pl.ds((z ^ d) * part, part)
        a_out[rows, :] = refs[d][:part, :]
        b_out[rows, :] = refs[d][part:, :]


def pair_join_kernel(which, own_ref, got_ref, out_ref):
    bit = which()
    part = own_ref.shape[0]
    out_ref[pl.ds(bit * part, part), :] = own_ref[...]
    out_ref[pl.ds((1 - bit) * part, part), :] = got_ref[...]


def unpack_kernel(row_total, *refs):
    (own_rows, other_rows, average_out, halves, centred) = refs[8:]
    core, x, y = core_bit(), x_bit(), y_bit()
    part = refs[0].shape[0]
    for h in range(2):
        base = 4 * part * h
        a_own, a_got, b_own, b_got = refs[4 * h : 4 * h + 4]
        halves[pl.ds(base + x * part, part), :] = a_own[...]
        halves[pl.ds(base + (1 - x) * part, part), :] = a_got[...]
        halves[pl.ds(base + (2 + y) * part, part), :] = b_own[...]
        halves[pl.ds(base + (3 - y) * part, part), :] = b_got[...]
    feat = own_rows.shape[1]
    blocks = feat // EDGE
    half_blocks = blocks // 2
    places = packed_places(blocks)
    row = lax.broadcasted_iota(jnp.int32, (EDGE, EDGE), 0)
    column = lax.broadcasted_iota(jnp.int32, (EDGE, EDGE), 1)
    lane = lax.broadcasted_iota(jnp.int32, (1, EDGE), 1)
    scale = 1.0 / row_total
    for side in range(2):

        @pl.when(core == side)
        def _():
            start = {}
            for owner in range(2):
                base = 0 if owner == side else 4 * part
                for i, j, first in places[owner]:
                    start[i, j] = base + first
            across, down = [], []
            for i in range(blocks):
                tail = halves[pl.ds(start[i, i] + EDGE - 8, 8), :]
                turned = pltpu.roll(tail, EDGE // 2, 1)
                average = jnp.where(lane < EDGE // 2, tail[7:8], turned[6:7]) * scale
                average_out[:, i * EDGE : (i + 1) * EDGE] = average
                wide = jnp.broadcast_to(average, (EDGE, EDGE))
                across.append(average)
                down.append(jnp.transpose(wide))
            squares = jnp.zeros((EDGE, EDGE), F32)

            def put(i, j, block):
                p, q = (i + half_blocks * side) % blocks, (j + half_blocks * side) % blocks
                centred[pl.ds(p * EDGE, EDGE), pl.ds(q * EDGE, EDGE)] = block

            for i in range(blocks):
                for j in range(i, blocks):
                    block = halves[pl.ds(start[i, j], EDGE), :] * scale - down[i] * across[j]
                    if i == j:
                        block = jnp.where(column >= row, block, jnp.transpose(block))
                        block = block + jnp.where(row == column, COV_EPS, 0.0)
                        squares = squares + block * block
                        put(i, i, block)
                    else:
                        squares = squares + 2.0 * (block * block)
                        put(i, j, block)
                        put(j, i, jnp.transpose(block))
            norm = jnp.sqrt(jnp.sum(jnp.sum(squares, axis=0, keepdims=True), axis=1, keepdims=True))
            factor = 1.0 / norm
            middle = feat // 2
            own_rows[...] = centred[:middle, :] * factor
            other_rows[:, :middle] = centred[middle:, middle:] * factor
            other_rows[:, middle:] = centred[middle:, :middle] * factor


def two(value):
    high = value.astype(BF16)
    return high, (value - high.astype(F32)).astype(BF16)


def times(left, high_ref, low_ref):
    high, low = two(left)
    return (
        jnp.dot(high, high_ref[...], preferred_element_type=F32)
        + jnp.dot(high, low_ref[...], preferred_element_type=F32)
        + jnp.dot(low, high_ref[...], preferred_element_type=F32)
    )


def load_full(own_ref, other_ref, high_ref, low_ref):
    middle = own_ref.shape[0]
    high_ref[:middle, :], low_ref[:middle, :] = two(own_ref[...])
    high_ref[middle:, :middle], low_ref[middle:, :middle] = two(other_ref[:, middle:])
    high_ref[middle:, middle:], low_ref[middle:, middle:] = two(other_ref[:, :middle])


def power_kernel(own_ref, other_ref, out_ref, high, low):
    load_full(own_ref, other_ref, high, low)
    square = times(own_ref[...], high, low)
    out_ref[...] = 2.25 * own_ref[...] - 1.5 * square + 0.25 * times(square, high, low)


def root_kernel(factor, first, last, own_ref, other_ref, root_ref, out_ref, high, low):
    load_full(own_ref, other_ref, high, low)
    root = root_ref[...] * -0.5 if first else root_ref[...]
    result = 1.5 * root - 0.5 * factor * own_ref[...] - 0.5 * times(root, high, low)
    if last:
        row = lax.broadcasted_iota(jnp.int32, result.shape, 0)
        column = lax.broadcasted_iota(jnp.int32, result.shape, 1)
        result = (result + jnp.where(row == column, 1.5 * factor, 0.0)).astype(BF16)
    out_ref[...] = result


def whiten_rows(rows, root_ref, offset):
    projected = jnp.dot(rows, root_ref[...], preferred_element_type=F32) - offset
    energy = jnp.sum(projected * projected, axis=1, keepdims=True)
    return (projected * lax.rsqrt(energy + UNIT_EPS)).astype(BF16)


def score_kernel(
    own_root, other_root, average_ref, values_ref, cluster_ref, piece_ref, ids_ref,
    out_ref, root, offset_ref, own_units, best,
):
    step = pl.program_id(0)
    core, me = core_bit(), lax.axis_index("grp")
    rows = values_ref.shape[0]

    @pl.when(step == 0)
    def _():
        middle, feat = own_root.shape
        root[pl.ds(core * middle, middle), :] = own_root[...]
        theirs = pl.ds((1 - core) * middle, middle)
        root[theirs, : feat // 2] = other_root[:, feat // 2 :]
        root[theirs, feat // 2 :] = other_root[:, : feat // 2]
        average = jnp.broadcast_to(average_ref[...], (16, feat))
        high, low = two(average)
        lowest = (average - high.astype(F32) - low.astype(F32)).astype(BF16)
        offset_ref[...] = (
            jnp.dot(high, root[...], preferred_element_type=F32)
            + jnp.dot(low, root[...], preferred_element_type=F32)
            + jnp.dot(lowest, root[...], preferred_element_type=F32)
        )[0:1]
        own_units[...] = whiten_rows(values_ref[...], root, offset_ref[...])
        best[...] = jnp.full(best.shape, -1.0, F32)

    units = whiten_rows(piece_ref[...], root, offset_ref[...])
    similar = lax.dot_general(
        own_units[...], units, (((1,), (1,)), ((), ())), preferred_element_type=F32
    )
    row = lax.broadcasted_iota(jnp.int32, (rows, rows), 0)
    column = lax.broadcasted_iota(jnp.int32, (rows, rows), 1)
    own_ids = jnp.transpose(jnp.broadcast_to(cluster_ref[...], (rows, rows)))
    same = (own_ids == ids_ref[0]) & ((row != column) | (step != me))
    best[...] = jnp.maximum(best[...], jnp.where(same, similar, -1.0))

    @pl.when(step == pl.num_programs(0) - 1)
    def _():
        out_ref[...] = jnp.max(jnp.transpose(best[...]), axis=0, keepdims=True)


def reduce_gram(values, blocks):
    length = lax.axis_size("grp") // 2
    part = -(-EDGE * (blocks * (blocks + 1) // 2) // (16 * length * 8)) * 8
    rows = part * length * 8
    swapped = swap(values, "rep", 1)
    a_keep, a_send, b_keep, b_send = call(
        gram_kernel,
        [shape(rows // 4, EDGE)] * 4,
        [values, swapped],
        flops=values.shape[0] * 2 * rows * EDGE * 2,
        scratch=[pltpu.VMEM((rows, EDGE), F32)],
    )
    a_got, b_got = swap(a_send, "grp", 1), swap(b_send, "rep", 2)
    second = [shape(rows // 8, EDGE)] * 2
    a_keep, a_send = call(functools.partial(halve_kernel, y_bit), second, [a_keep, a_got])
    b_keep, b_send = call(functools.partial(halve_kernel, x_bit), second, [b_keep, b_got])
    a_got, b_got = swap(a_send, "rep", 2), swap(b_send, "grp", 1)
    pieces = call(
        functools.partial(line_split_kernel, length),
        [shape(2 * part, EDGE)] * length,
        [a_keep, a_got, b_keep, b_got],
    )
    got = [swap(pieces[d], "grp", 2 * d) for d in range(1, length)]
    (total,) = call(line_sum_kernel, [shape(2 * part, EDGE)], [pieces[0]] + got)
    got = [swap(total, "grp", 2 * d) for d in range(1, length)]
    a_own, b_own = call(functools.partial(line_join_kernel, length), second, [total] + got)
    a_got, b_got = swap(a_own, "rep", 2), swap(b_own, "grp", 1)
    third = [shape(rows // 4, EDGE)]
    (a_own,) = call(functools.partial(pair_join_kernel, y_bit), third, [a_own, a_got])
    (b_own,) = call(functools.partial(pair_join_kernel, x_bit), third, [b_own, b_got])
    a_got, b_got = swap(a_own, "grp", 1), swap(b_own, "rep", 2)
    own = [a_own, a_got, b_own, b_got]
    return own + [swap(piece, "rep", 1) for piece in own]


def inverse_root_slabs(own, other, feat):
    middle = feat // 2
    full = [pltpu.VMEM((feat, feat), BF16)] * 2
    flops = 2 * 3 * middle * feat * feat
    slab = [shape(middle, feat)]
    root, factor = own, 1.5
    (power,) = call(power_kernel, slab, [own, other], 2 * flops, full)
    own, other = power, swap(power, "rep", 1)
    for step in range(1, STEPS):
        last = step == STEPS - 1
        if not last:
            (power,) = call(power_kernel, slab, [own, other], 2 * flops, full)
            power_other = swap(power, "rep", 1)
        (root,) = call(
            functools.partial(root_kernel, factor, step == 1, last),
            [shape(middle, feat, BF16 if last else F32)],
            [own, other, root],
            flops,
            full,
        )
        factor = 1.5 * factor
        if not last:
            own, other = power, power_other
    return root, swap(root, "rep", 1)


def local(embeddings, scales, cluster, cluster_rank):
    row_count, feat = embeddings.shape
    group = lax.axis_size("grp")
    row_total = row_count * group * lax.axis_size("rep")
    (values,) = call(dequantize_kernel, [shape(row_count, feat, BF16)], [embeddings, scales])
    gathered = lax.all_gather(values, "grp", axis=0, tiled=True)
    ids = lax.all_gather(cluster, "grp", axis=0, tiled=True).reshape(group, 1, row_count)
    pieces = reduce_gram(values, feat // EDGE)
    middle = feat // 2
    own, other, average = call(
        functools.partial(unpack_kernel, row_total),
        [shape(middle, feat), shape(middle, feat), shape(1, feat)],
        pieces,
        scratch=[pltpu.VMEM((8 * pieces[0].shape[0], EDGE), F32), pltpu.VMEM((feat, feat), F32)],
    )
    own_root, other_root = inverse_root_slabs(own, other, feat)
    full = lambda *dims: pl.BlockSpec(dims, lambda i: (0,) * len(dims))
    best = pl.pallas_call(
        score_kernel,
        grid=(group,),
        out_shape=shape(1, row_count),
        in_specs=[
            full(middle, feat),
            full(middle, feat),
            full(1, feat),
            full(row_count, feat),
            full(1, row_count),
            pl.BlockSpec((row_count, feat), lambda i: (i, 0)),
            pl.BlockSpec((1, 1, row_count), lambda i: (i, 0, 0)),
        ],
        out_specs=full(1, row_count),
        scratch_shapes=[
            pltpu.VMEM((feat, feat), BF16),
            pltpu.VMEM((1, feat), F32),
            pltpu.VMEM((row_count, feat), BF16),
            pltpu.VMEM((row_count, row_count), F32),
        ],
        compiler_params=pltpu.CompilerParams(vmem_limit_bytes=VMEM_BYTES),
        cost_estimate=pl.CostEstimate(
            flops=2 * group * row_count * feat * (feat + row_count),
            bytes_accessed=2 * group * row_count * feat,
            transcendentals=0,
        ),
    )(own_root, other_root, average, values, cluster.reshape(1, row_count), gathered, ids)
    return best.reshape(row_count)


def solution(mesh):
    placed = (
        P(("grp", "rep"), None),
        P(("grp", "rep"), None),
        P(("grp", "rep")),
        P(("grp", "rep")),
    )
    return jax.shard_map(
        local, mesh=mesh, in_specs=placed, out_specs=P(("grp", "rep")), check_vma=False
    )
```

```python
import functools

import jax
import jax.numpy as jnp
from jax import lax
from jax.experimental import pallas as pl
from jax.experimental.pallas import tpu as pltpu
from jax.sharding import PartitionSpec as P

STEPS = 5
COV_EPS = 0.001
UNIT_EPS = 1e-06
EDGE = 128
F32 = jnp.float32
BF16 = jnp.bfloat16
SMALL_BYTES = 6 * 2**20
UNPACK_BYTES = 14 * 2**20
NEWTON_BYTES = 14 * 2**20
SCORE_BYTES = 16 * 2**20
IN_PIECES_BYTES = 8 * 2**20
CUTS = 4
HALVES = 2
SHRINK = 1


def swap(array, axis, bit):
    size = lax.axis_size(axis)
    return lax.ppermute(array, axis, [(i, i ^ bit) for i in range(size)])


def whole(count):
    return [pl.BlockSpec(memory_space=pltpu.VMEM)] * count


def call(kernel, outs, ins, flops=0, scratch=(), limit=SMALL_BYTES, after=()):
    moved = sum(a.size * a.dtype.itemsize for a in list(ins) + list(outs))
    return pl.pallas_call(
        kernel,
        out_shape=outs,
        in_specs=whole(len(ins)) + [pl.BlockSpec(memory_space=pl.ANY)] * len(after),
        out_specs=whole(len(outs)),
        scratch_shapes=list(scratch),
        compiler_params=pltpu.CompilerParams(vmem_limit_bytes=limit),
        cost_estimate=pl.CostEstimate(flops=flops // SHRINK, bytes_accessed=moved // SHRINK, transcendentals=0),
    )(*ins, *after)


def shape(rows, columns, dtype=F32):
    return jax.ShapeDtypeStruct((rows, columns), dtype)


def core_bit():
    return lax.axis_index("rep") % 2


def y_bit():
    return lax.axis_index("rep") // 2


def x_bit():
    return lax.axis_index("grp") % 2


def z_pos():
    return lax.axis_index("grp") // 2


def block_rows(blocks):
    total = blocks * (blocks + 1) // 2
    halves, room = ([], []), total // 2
    for i in range(blocks):
        if blocks - i <= room:
            halves[0].append(i)
            room -= blocks - i
        else:
            halves[1].append(i)
    return halves


def packed_places(blocks):
    places = []
    for rows in block_rows(blocks):
        pairs = [(i, j) for i in rows for j in range(i, blocks)]
        places.append([(i, j, EDGE * k) for k, (i, j) in enumerate(pairs)])
    return places


def dequantize_kernel(emb_ref, scale_ref, out_ref):
    blocks = scale_ref.shape[1]
    width = emb_ref.shape[1] // blocks
    for b in range(blocks):
        columns = pl.ds(b * width, width)
        out_ref[:, columns] = (
            emb_ref[:, columns].astype(F32) * scale_ref[:, b : b + 1]
        ).astype(BF16)


def gram_kernel(own_ref, other_ref, a_keep, a_send, b_keep, b_send, packed):
    blocks = own_ref.shape[1] // EDGE
    contract = (((0,), (0,)), ((), ()))
    core, x, y = core_bit(), x_bit(), y_bit()
    row = lax.broadcasted_iota(jnp.int32, (EDGE, EDGE), 0)
    column = lax.broadcasted_iota(jnp.int32, (EDGE, EDGE), 1)
    half = EDGE // 2
    places = packed_places(blocks)
    if packed.shape[0] > EDGE * len(places[0]):
        packed[...] = jnp.zeros_like(packed)
    for side in range(2):

        @pl.when(core == side)
        def _():
            first = {(i, j): start for i, j, start in places[side]}
            for i in block_rows(blocks)[side]:
                mine = pl.ds(i * EDGE, EDGE)
                rest = pl.ds(i * EDGE, (blocks - i) * EDGE)
                total = lax.dot_general(
                    own_ref[:, mine], own_ref[:, rest], contract, preferred_element_type=F32
                ) + lax.dot_general(
                    other_ref[:, mine], other_ref[:, rest], contract, preferred_element_type=F32
                )
                sums = jnp.sum(own_ref[:, mine].astype(F32), axis=0, keepdims=True) + jnp.sum(
                    other_ref[:, mine].astype(F32), axis=0, keepdims=True
                )
                turned = pltpu.roll(jnp.broadcast_to(sums, (8, EDGE)), half, 1)[0:1]
                diagonal = total[:, :EDGE]
                diagonal = jnp.where((row == EDGE - 1) & (column < half), sums, diagonal)
                diagonal = jnp.where((row == EDGE - 2) & (column < half), turned, diagonal)
                packed[pl.ds(first[i, i], EDGE), :] = diagonal
                for j in range(i + 1, blocks):
                    packed[pl.ds(first[i, j], EDGE), :] = total[
                        :, (j - i) * EDGE : (j - i + 1) * EDGE
                    ]

    part = a_keep.shape[0]
    a_keep[...] = packed[pl.ds(x * part, part), :]
    a_send[...] = packed[pl.ds((1 - x) * part, part), :]
    b_keep[...] = packed[pl.ds((2 + y) * part, part), :]
    b_send[...] = packed[pl.ds((3 - y) * part, part), :]


def halve_kernel(which, keep_ref, got_ref, *refs):
    keep_out, send_out = refs[-2:]
    bit = which()
    part = keep_out.shape[0]
    mine, theirs = pl.ds(bit * part, part), pl.ds((1 - bit) * part, part)
    keep_out[...] = keep_ref[mine, :] + got_ref[mine, :]
    send_out[...] = keep_ref[theirs, :] + got_ref[theirs, :]


def line_split_kernel(length, a_keep, a_got, b_keep, b_got, *refs):
    outs = refs[-length:]
    z = z_pos()
    part = a_keep.shape[0] // length
    for d in range(length):
        rows = pl.ds((z ^ d) * part, part)
        outs[d][:part, :] = a_keep[rows, :] + a_got[rows, :]
        outs[d][part:, :] = b_keep[rows, :] + b_got[rows, :]


def line_sum_kernel(*refs):
    total = refs[0][...]
    for ref in refs[1:-1]:
        total = total + ref[...]
    refs[-1][...] = total


def line_join_kernel(length, *refs):
    z = z_pos()
    a_out, b_out = refs[-2:]
    part = a_out.shape[0] // length
    for d in range(length):
        rows = pl.ds((z ^ d) * part, part)
        a_out[rows, :] = refs[d][:part, :]
        b_out[rows, :] = refs[d][part:, :]


def pair_join_kernel(which, own_ref, got_ref, out_ref):
    bit = which()
    part = own_ref.shape[0]
    out_ref[pl.ds(bit * part, part), :] = own_ref[...]
    out_ref[pl.ds((1 - bit) * part, part), :] = got_ref[...]


def unpack_kernel(row_total, *refs):
    own_rows, average_out, *pairs, halves, centred = refs[-2 * CUTS - 4 :]
    own_pair, other_pair = pairs[:CUTS], pairs[CUTS:]
    core, x, y = core_bit(), x_bit(), y_bit()
    part = refs[0].shape[0]
    for h in range(2):
        base = 4 * part * h
        a_own, a_got, b_own, b_got = refs[4 * h : 4 * h + 4]
        halves[pl.ds(base + x * part, part), :] = a_own[...]
        halves[pl.ds(base + (1 - x) * part, part), :] = a_got[...]
        halves[pl.ds(base + (2 + y) * part, part), :] = b_own[...]
        halves[pl.ds(base + (3 - y) * part, part), :] = b_got[...]
    feat = own_rows.shape[1]
    blocks = feat // EDGE
    half_blocks = blocks // 2
    places = packed_places(blocks)
    row = lax.broadcasted_iota(jnp.int32, (EDGE, EDGE), 0)
    column = lax.broadcasted_iota(jnp.int32, (EDGE, EDGE), 1)
    lane = lax.broadcasted_iota(jnp.int32, (1, EDGE), 1)
    scale = 1.0 / row_total
    for side in range(2):

        @pl.when(core == side)
        def _():
            start = {}
            for owner in range(2):
                base = 0 if owner == side else 4 * part
                for i, j, first in places[owner]:
                    start[i, j] = base + first
            across, down = [], []
            for i in range(blocks):
                tail = halves[pl.ds(start[i, i] + EDGE - 8, 8), :]
                turned = pltpu.roll(tail, EDGE // 2, 1)
                average = jnp.where(lane < EDGE // 2, tail[7:8], turned[6:7]) * scale
                average_out[:, i * EDGE : (i + 1) * EDGE] = average
                wide = jnp.broadcast_to(average, (EDGE, EDGE))
                across.append(average)
                down.append(jnp.transpose(wide))
            squares = jnp.zeros((EDGE, EDGE), F32)

            def put(i, j, block):
                p, q = (i + half_blocks * side) % blocks, (j + half_blocks * side) % blocks
                centred[pl.ds(p * EDGE, EDGE), pl.ds(q * EDGE, EDGE)] = block

            for i in range(blocks):
                for j in range(i, blocks):
                    block = halves[pl.ds(start[i, j], EDGE), :] * scale - down[i] * across[j]
                    if i == j:
                        block = jnp.where(column >= row, block, jnp.transpose(block))
                        block = block + jnp.where(row == column, COV_EPS, 0.0)
                        squares = squares + block * block
                        put(i, i, block)
                    else:
                        squares = squares + 2.0 * (block * block)
                        put(i, j, block)
                        put(j, i, jnp.transpose(block))
            norm = jnp.sqrt(jnp.sum(jnp.sum(squares, axis=0, keepdims=True), axis=1, keepdims=True))
            factor = 1.0 / norm
            middle = feat // 2
            own = centred[:middle, :] * factor
            own_rows[...] = own
            split_into(own, own_pair)
            theirs = jnp.concatenate([centred[middle:, middle:], centred[middle:, :middle]], axis=1)
            split_into(theirs * factor, other_pair)


def two(value):
    high = value.astype(BF16)
    return high, (value - high.astype(F32)).astype(BF16)


def split_into(value, pair_refs):
    high, low = two(value)
    both = jnp.concatenate([high, low], axis=0)
    rows = both.shape[0] // len(pair_refs)
    for k, ref in enumerate(pair_refs):
        ref[...] = both[k * rows : (k + 1) * rows, :]


def load_full(own_refs, other_refs, high_ref, low_ref):
    middle = high_ref.shape[0] // 2
    rows = own_refs[0].shape[0]
    for k, (own_ref, other_ref) in enumerate(zip(own_refs, other_refs)):
        full = high_ref if k * rows < middle else low_ref
        first = k * rows % middle
        mine = pl.ds(first, rows)
        theirs = pl.ds(middle + first, rows)
        full[mine, :] = own_ref[...]
        full[theirs, :middle] = other_ref[:, middle:]
        full[theirs, middle:] = other_ref[:, :middle]


def times(high, low, high_ref, low_ref):
    return (
        jnp.dot(high, high_ref[...], preferred_element_type=F32)
        + jnp.dot(high, low_ref[...], preferred_element_type=F32)
        + jnp.dot(low, high_ref[...], preferred_element_type=F32)
    )


def power_kernel(own_ref, *refs):
    pair, other = refs[:CUTS], refs[CUTS : 2 * CUTS]
    out_ref, *out_pair, high, low = refs[-CUTS - 3 :]
    load_full(pair, other, high, low)
    middle = own_ref.shape[0]
    square = times(high[:middle, :], low[:middle, :], high, low)
    cube = times(*two(square), high, low)
    result = 2.25 * own_ref[...] - 1.5 * square + 0.25 * cube
    out_ref[...] = result
    split_into(result, out_pair)


def root_kernel(factor, first, last, own_ref, root_ref, *refs):
    pair, other = refs[:CUTS], refs[CUTS : 2 * CUTS]
    out_ref, high, low = refs[-3:]
    load_full(pair, other, high, low)
    root = root_ref[...] * -0.5 if first else root_ref[...]
    result = 1.5 * root - 0.5 * factor * own_ref[...] - 0.5 * times(*two(root), high, low)
    if last:
        row = lax.broadcasted_iota(jnp.int32, result.shape, 0)
        column = lax.broadcasted_iota(jnp.int32, result.shape, 1)
        result = (result + jnp.where(row == column, 1.5 * factor, 0.0)).astype(BF16)
    out_ref[...] = result


def whiten_rows(rows, root_ref, offset):
    projected = jnp.dot(rows, root_ref[...], preferred_element_type=F32) - offset
    energy = jnp.sum(projected * projected, axis=1, keepdims=True)
    return (projected * lax.rsqrt(energy + UNIT_EPS)).astype(BF16)


def build_root(own_root, other_root, average_ref, root, offset_ref):
    core = core_bit()
    middle, feat = own_root.shape
    root[pl.ds(core * middle, middle), :] = own_root[...]
    theirs = pl.ds((1 - core) * middle, middle)
    root[theirs, : feat // 2] = other_root[:, feat // 2 :]
    root[theirs, feat // 2 :] = other_root[:, : feat // 2]
    average = jnp.broadcast_to(average_ref[...], (16, feat))
    high, low = two(average)
    lowest = (average - high.astype(F32) - low.astype(F32)).astype(BF16)
    offset_ref[...] = (
        jnp.dot(high, root[...], preferred_element_type=F32)
        + jnp.dot(low, root[...], preferred_element_type=F32)
        + jnp.dot(lowest, root[...], preferred_element_type=F32)
    )[0:1]


def similarity(own_units, units):
    return lax.dot_general(
        own_units, units, (((1,), (1,)), ((), ())), preferred_element_type=F32
    )


def column_ids(ids):
    return jnp.transpose(jnp.broadcast_to(ids, (ids.shape[1], ids.shape[1])))


def off_diagonal(rows):
    row = lax.broadcasted_iota(jnp.int32, (rows, rows), 0)
    return row != lax.broadcasted_iota(jnp.int32, (rows, rows), 1)


def highest(best):
    return jnp.max(jnp.transpose(best), axis=0, keepdims=True)


def score_pieces_kernel(sources, own_root, other_root, average_ref, ids_ref, values_ref, *refs):
    *parts, out_ref, root, offset_ref = refs
    me = lax.axis_index("grp")
    build_root(own_root, other_root, average_ref, root, offset_ref)
    offset = offset_ref[...]
    own_units = whiten_rows(values_ref[...], root, offset)
    own_ids = column_ids(ids_ref[0:1, :])
    same = (own_ids == ids_ref[0:1, :]) & off_diagonal(values_ref.shape[0])
    best = jnp.where(same, similarity(own_units, own_units), -1.0)
    for source in sources(me):
        count = values_ref.shape[0] // parts[0].shape[0]
        piece, parts = jnp.concatenate([part[...] for part in parts[:count]], axis=0), parts[count:]
        similar = similarity(own_units, whiten_rows(piece, root, offset))
        same = own_ids == ids_ref[pl.ds(source ^ me, 1), :]
        best = jnp.maximum(best, jnp.where(same, similar, -1.0))
    out_ref[...] = highest(best)


def score_kernel(
    own_root, other_root, average_ref, ids_ref, values_ref, piece_ref,
    out_ref, root, offset_ref, own_units, best,
):
    step = pl.program_id(0)
    me = lax.axis_index("grp")

    @pl.when(step == 0)
    def _():
        build_root(own_root, other_root, average_ref, root, offset_ref)
        own_units[...] = whiten_rows(values_ref[...], root, offset_ref[...])
        best[...] = jnp.full(best.shape, -1.0, F32)

    units = whiten_rows(piece_ref[...], root, offset_ref[...])
    same = column_ids(ids_ref[0:1, :]) == ids_ref[pl.ds(step ^ me, 1), :]
    same = same & (off_diagonal(values_ref.shape[0]) | (step != me))
    best[...] = jnp.maximum(best[...], jnp.where(same, similarity(own_units[...], units), -1.0))

    @pl.when(step == pl.num_programs(0) - 1)
    def _():
        out_ref[...] = highest(best[...])


def pick_kernel(limit, near_ref, far_ref, *refs):
    z = z_pos()
    outs = refs[-HALVES:]
    rows = outs[0].shape[0]

    def put(ref):
        for k, out in enumerate(outs):
            out[...] = ref[pl.ds(k * rows, rows), :]

    pl.when(z < limit)(lambda: put(near_ref))
    pl.when(z >= limit)(lambda: put(far_ref))


def hold_kernel(*refs):
    count = (len(refs) - 1) // 2
    for source, out in zip(refs[:count], refs[len(refs) - count :]):
        out[...] = source[...]


def hold(arrays, after):
    outs = [jax.ShapeDtypeStruct(array.shape, array.dtype) for array in arrays]
    return call(hold_kernel, outs, arrays, after=after)


def join_kernel(first_ref, second_ref, out_ref):
    rows = first_ref.shape[0]
    out_ref[:rows, :] = first_ref[...]
    out_ref[rows:, :] = second_ref[...]


class Ids:
    def __init__(self, cluster):
        self.size = lax.axis_size("grp")
        self.held = cluster.reshape(1, cluster.shape[0])

    def step(self):
        count, columns = self.held.shape
        if count < self.size:
            got = swap(self.held, "grp", count)
            (self.held,) = call(
                join_kernel, [shape(2 * count, columns, jnp.int32)], [self.held, got]
            )
        return [self.held]

    def all(self):
        while self.held.shape[0] < self.size:
            self.step()
        return self.held


class Gather:
    def __init__(self, values):
        self.length = lax.axis_size("grp") // 2
        self.right = {0: values}
        self.left = {0: values}
        self.slots, self.across = {}, {}

    def along(self, t, after=()):
        size, length = 2 * self.length, self.length
        right, left = self.right[t - 1], self.left[t - 1]
        if after:
            right, left = hold([right, left], after)
        self.right[t] = lax.ppermute(
            right, "grp", [(g, g - 2) for g in range(size) if 1 <= g // 2 <= length - t]
        )
        self.left[t] = lax.ppermute(
            left, "grp", [(g, g + 2) for g in range(size) if t - 1 <= g // 2 <= length - 2]
        )
        return [self.right[t], self.left[t]]

    def pick(self, t, after=()):
        rows, feat = self.right[0].shape
        self.slots[t] = call(
            functools.partial(pick_kernel, self.length - t),
            [shape(rows // HALVES, feat, BF16)] * HALVES,
            [self.right[t], self.left[self.length - t]],
            after=after,
        )
        return list(self.slots[t])

    def cross(self, t, k, after):
        (held,) = hold([self.slots[t][k]], after) if after else [self.slots[t][k]]
        got = swap(held, "grp", 1)
        self.across.setdefault(t, {})[k] = got
        return [got]

    def pieces(self):
        column = [self.slots[t][k] for t in range(1, self.length) for k in range(HALVES)]
        return column + [
            self.across[t][k] for t in range(self.length) for k in range(len(self.across[t]))
        ]

    def sources(self, me):
        z, x = me // 2, me % 2
        column = [((z + t) % self.length) * 2 for t in range(self.length)]
        return [c + x for c in column[1:]] + [c + 1 - x for c in column]


def best_cosines(own_root, other_root, average, ids, values, gathered):
    rows, feat = values.shape
    group = lax.axis_size("grp")
    scratch = [pltpu.VMEM((feat, feat), BF16), pltpu.VMEM((1, feat), F32)]
    flops = 2 * group * rows * feat * (feat + rows)
    ins = [own_root, other_root, average, ids, values]
    if isinstance(gathered, Gather):
        kernel = functools.partial(score_pieces_kernel, gathered.sources)
        (best,) = call(kernel, [shape(1, rows)], ins + gathered.pieces(), flops, scratch, SCORE_BYTES)
        return best
    full = lambda array: pl.BlockSpec(array.shape, lambda i: (0, 0))
    return pl.pallas_call(
        score_kernel,
        grid=(group,),
        out_shape=shape(1, rows),
        in_specs=[full(array) for array in ins] + [pl.BlockSpec((rows, feat), lambda i: (i, 0))],
        out_specs=pl.BlockSpec((1, rows), lambda i: (0, 0)),
        scratch_shapes=scratch + [pltpu.VMEM((rows, feat), BF16), pltpu.VMEM((rows, rows), F32)],
        compiler_params=pltpu.CompilerParams(vmem_limit_bytes=SCORE_BYTES),
        cost_estimate=pl.CostEstimate(
            flops=flops, bytes_accessed=2 * group * rows * feat, transcendentals=0
        ),
    )(*ins, gathered)


def reduce_gram(values, blocks, gather, ids):
    length = lax.axis_size("grp") // 2
    part = -(-EDGE * (blocks * (blocks + 1) // 2) // (16 * length * 8)) * 8
    rows = part * length * 8
    swapped = swap(values, "rep", 1)
    a_keep, a_send, b_keep, b_send = call(
        gram_kernel,
        [shape(rows // 4, EDGE)] * 4,
        [values, swapped],
        flops=values.shape[0] * 2 * rows * EDGE * 2,
        scratch=[pltpu.VMEM((rows, EDGE), F32)],
    )
    a_got, b_got = swap(a_send, "grp", 1), swap(b_send, "rep", 2)
    second = [shape(rows // 8, EDGE)] * 2
    wait = ids.step()
    a_keep, a_send = call(functools.partial(halve_kernel, y_bit), second, [a_keep, a_got], after=wait)
    b_keep, b_send = call(functools.partial(halve_kernel, x_bit), second, [b_keep, b_got], after=wait)
    wait = ids.step()
    a_got, b_got = swap(a_send, "rep", 2), swap(b_send, "grp", 1)
    pieces = call(
        functools.partial(line_split_kernel, length),
        [shape(2 * part, EDGE)] * length,
        [a_keep, a_got, b_keep, b_got],
        after=wait + (gather.along(1) if gather else []),
    )
    got = [swap(pieces[d], "grp", 2 * d) for d in range(1, length)]
    (total,) = call(line_sum_kernel, [shape(2 * part, EDGE)], [pieces[0]] + got)
    got = [swap(total, "grp", 2 * d) for d in range(1, length)]
    wait = ids.step()
    if gather:
        gather.slots[0] = hold([values], [pieces[0]])
        wait = wait + gather.cross(0, 0, ())
    a_own, b_own = call(
        functools.partial(line_join_kernel, length), second, [total] + got, after=wait
    )
    wait = gather.along(2, [a_own]) if gather else []
    a_got, b_got = swap(a_own, "rep", 2), swap(b_own, "grp", 1)
    third = [shape(rows // 4, EDGE)]
    (a_own,) = call(functools.partial(pair_join_kernel, y_bit), third, [a_own, a_got])
    (b_own,) = call(functools.partial(pair_join_kernel, x_bit), third, [b_own, b_got])
    a_got, b_got = swap(a_own, "grp", 1), swap(b_own, "rep", 2)
    own = [a_own, a_got, b_own, b_got]
    return own + [swap(piece, "rep", 1) for piece in own], wait


def inverse_root_slabs(own, pair, other, feat, gather):
    middle = feat // 2
    full = [pltpu.VMEM((feat, feat), BF16)] * 2
    flops = 2 * 3 * middle * feat * feat
    outs = [shape(middle, feat)] + [shape(2 * middle // CUTS, feat, BF16)] * CUTS
    root, factor, after = own, 1.5, []
    crossings = [(1, 0), (1, 1), (3, 0), (3, 1)]
    if gather:
        gather.pick(2, [own])
        wait = gather.along(3)
        wait = gather.cross(2, 0, ()) + gather.cross(2, 1, ()) + gather.pick(1) + gather.pick(3)
    for step in range(STEPS):
        last = step == STEPS - 1
        if not last:
            power, *power_pair = call(
                power_kernel, outs, [own] + pair + other, 2 * flops, full, NEWTON_BYTES, after
            )
            power_other = [swap(piece, "rep", 1) for piece in power_pair]
        if step > 0:
            waits = gather.cross(*crossings[step - 1], [early if last else own]) if gather else []
            (root,) = call(
                functools.partial(root_kernel, factor, step == 1, last),
                [shape(middle, feat, BF16 if last else F32)],
                [own, root] + pair + other,
                flops,
                full,
                NEWTON_BYTES,
                waits,
            )
            factor, after = 1.5 * factor, [root]
            early = root if step < STEPS - 2 else early
        elif gather:
            after = wait
        if not last:
            own, pair, other = power, power_pair, power_other
    return root, swap(root, "rep", 1)


def local(embeddings, scales, cluster, cluster_rank):
    row_count, feat = embeddings.shape
    group = lax.axis_size("grp")
    row_total = row_count * group * lax.axis_size("rep")
    (values,) = call(dequantize_kernel, [shape(row_count, feat, BF16)], [embeddings, scales])
    ids = Ids(cluster)
    gather, gathered = None, None
    if group * values.size * values.dtype.itemsize <= IN_PIECES_BYTES:
        gather = Gather(values)
    else:
        gathered = lax.all_gather(values, "grp", axis=0, tiled=True)
    pieces, wait = reduce_gram(values, feat // EDGE, gather, ids)
    middle = feat // 2
    pair_shapes = [shape(2 * middle // CUTS, feat, BF16)] * (2 * CUTS)
    own, average, *pairs = call(
        functools.partial(unpack_kernel, row_total),
        [shape(middle, feat), shape(1, feat)] + pair_shapes,
        pieces,
        after=wait,
        scratch=[pltpu.VMEM((8 * pieces[0].shape[0], EDGE), F32), pltpu.VMEM((feat, feat), F32)],
        limit=UNPACK_BYTES,
    )
    own_root, other_root = inverse_root_slabs(own, pairs[:CUTS], pairs[CUTS:], feat, gather)
    best = best_cosines(own_root, other_root, average, ids.all(), values, gather or gathered)
    return best.reshape(row_count)


def solution(mesh):
    placed = (
        P(("grp", "rep"), None),
        P(("grp", "rep"), None),
        P(("grp", "rep")),
        P(("grp", "rep")),
    )
    return jax.shard_map(
        local, mesh=mesh, in_specs=placed, out_specs=P(("grp", "rep")), check_vma=False
    )
```

```python
import functools

import jax
import jax.numpy as jnp
from jax import lax
from jax.experimental import pallas as pl
from jax.experimental.pallas import tpu as pltpu
from jax.sharding import PartitionSpec as P

STEPS = 5
COV_EPS = 0.001
UNIT_EPS = 1e-06
EDGE = 128
F32 = jnp.float32
BF16 = jnp.bfloat16
SMALL_BYTES = 6 * 2**20
UNPACK_BYTES = 14 * 2**20
NEWTON_BYTES = 14 * 2**20
SCORE_BYTES = 16 * 2**20
IN_PIECES_BYTES = 8 * 2**20
CUTS = 4
SHRINK = 1


def swap(array, axis, bit):
    size = lax.axis_size(axis)
    return lax.ppermute(array, axis, [(i, i ^ bit) for i in range(size)])


def whole(count):
    return [pl.BlockSpec(memory_space=pltpu.VMEM)] * count


def call(kernel, outs, ins, flops=0, scratch=(), limit=SMALL_BYTES, after=()):
    moved = sum(a.size * a.dtype.itemsize for a in list(ins) + list(outs))
    return pl.pallas_call(
        kernel,
        out_shape=outs,
        in_specs=whole(len(ins)) + [pl.BlockSpec(memory_space=pl.ANY)] * len(after),
        out_specs=whole(len(outs)),
        scratch_shapes=list(scratch),
        compiler_params=pltpu.CompilerParams(vmem_limit_bytes=limit),
        cost_estimate=pl.CostEstimate(flops=flops // SHRINK, bytes_accessed=moved // SHRINK, transcendentals=0),
    )(*ins, *after)


def shape(rows, columns, dtype=F32):
    return jax.ShapeDtypeStruct((rows, columns), dtype)


def core_bit():
    return lax.axis_index("rep") % 2


def y_bit():
    return lax.axis_index("rep") // 2


def x_bit():
    return lax.axis_index("grp") % 2


def z_pos():
    return lax.axis_index("grp") // 2


def block_rows(blocks):
    total = blocks * (blocks + 1) // 2
    halves, room = ([], []), total // 2
    for i in range(blocks):
        if blocks - i <= room:
            halves[0].append(i)
            room -= blocks - i
        else:
            halves[1].append(i)
    return halves


def packed_places(blocks):
    places = []
    for rows in block_rows(blocks):
        pairs = [(i, j) for i in rows for j in range(i, blocks)]
        places.append([(i, j, EDGE * k) for k, (i, j) in enumerate(pairs)])
    return places


def dequantize_kernel(emb_ref, scale_ref, out_ref):
    blocks = scale_ref.shape[1]
    width = emb_ref.shape[1] // blocks
    for b in range(blocks):
        columns = pl.ds(b * width, width)
        out_ref[:, columns] = (
            emb_ref[:, columns].astype(F32) * scale_ref[:, b : b + 1]
        ).astype(BF16)


def gram_kernel(own_ref, other_ref, a_keep, a_send, b_keep, b_send, packed):
    blocks = own_ref.shape[1] // EDGE
    contract = (((0,), (0,)), ((), ()))
    core, x, y = core_bit(), x_bit(), y_bit()
    row = lax.broadcasted_iota(jnp.int32, (EDGE, EDGE), 0)
    column = lax.broadcasted_iota(jnp.int32, (EDGE, EDGE), 1)
    half = EDGE // 2
    places = packed_places(blocks)
    if packed.shape[0] > EDGE * len(places[0]):
        packed[...] = jnp.zeros_like(packed)
    for side in range(2):

        @pl.when(core == side)
        def _():
            first = {(i, j): start for i, j, start in places[side]}
            for i in block_rows(blocks)[side]:
                mine = pl.ds(i * EDGE, EDGE)
                rest = pl.ds(i * EDGE, (blocks - i) * EDGE)
                total = lax.dot_general(
                    own_ref[:, mine], own_ref[:, rest], contract, preferred_element_type=F32
                ) + lax.dot_general(
                    other_ref[:, mine], other_ref[:, rest], contract, preferred_element_type=F32
                )
                sums = jnp.sum(own_ref[:, mine].astype(F32), axis=0, keepdims=True) + jnp.sum(
                    other_ref[:, mine].astype(F32), axis=0, keepdims=True
                )
                turned = pltpu.roll(jnp.broadcast_to(sums, (8, EDGE)), half, 1)[0:1]
                diagonal = total[:, :EDGE]
                diagonal = jnp.where((row == EDGE - 1) & (column < half), sums, diagonal)
                diagonal = jnp.where((row == EDGE - 2) & (column < half), turned, diagonal)
                packed[pl.ds(first[i, i], EDGE), :] = diagonal
                for j in range(i + 1, blocks):
                    packed[pl.ds(first[i, j], EDGE), :] = total[
                        :, (j - i) * EDGE : (j - i + 1) * EDGE
                    ]

    part = a_keep.shape[0]
    a_keep[...] = packed[pl.ds(x * part, part), :]
    a_send[...] = packed[pl.ds((1 - x) * part, part), :]
    b_keep[...] = packed[pl.ds((2 + y) * part, part), :]
    b_send[...] = packed[pl.ds((3 - y) * part, part), :]


def halve_kernel(which, keep_ref, got_ref, *refs):
    keep_out, send_out = refs[-2:]
    bit = which()
    part = keep_out.shape[0]
    mine, theirs = pl.ds(bit * part, part), pl.ds((1 - bit) * part, part)
    keep_out[...] = keep_ref[mine, :] + got_ref[mine, :]
    send_out[...] = keep_ref[theirs, :] + got_ref[theirs, :]


def line_split_kernel(length, a_keep, a_got, b_keep, b_got, *refs):
    outs = refs[-length:]
    z = z_pos()
    part = a_keep.shape[0] // length
    for d in range(length):
        rows = pl.ds((z ^ d) * part, part)
        outs[d][:part, :] = a_keep[rows, :] + a_got[rows, :]
        outs[d][part:, :] = b_keep[rows, :] + b_got[rows, :]


def line_sum_kernel(*refs):
    total = refs[0][...]
    for ref in refs[1:-1]:
        total = total + ref[...]
    refs[-1][...] = total


def line_join_kernel(length, *refs):
    z = z_pos()
    a_out, b_out = refs[-2:]
    part = a_out.shape[0] // length
    for d in range(length):
        rows = pl.ds((z ^ d) * part, part)
        a_out[rows, :] = refs[d][:part, :]
        b_out[rows, :] = refs[d][part:, :]


def pair_join_kernel(which, own_ref, got_ref, out_ref):
    bit = which()
    part = own_ref.shape[0]
    out_ref[pl.ds(bit * part, part), :] = own_ref[...]
    out_ref[pl.ds((1 - bit) * part, part), :] = got_ref[...]


def unpack_kernel(row_total, *refs):
    own_rows, average_out, *pairs, halves, centred = refs[-2 * CUTS - 4 :]
    own_pair, other_pair = pairs[:CUTS], pairs[CUTS:]
    core, x, y = core_bit(), x_bit(), y_bit()
    part = refs[0].shape[0]
    for h in range(2):
        base = 4 * part * h
        a_own, a_got, b_own, b_got = refs[4 * h : 4 * h + 4]
        halves[pl.ds(base + x * part, part), :] = a_own[...]
        halves[pl.ds(base + (1 - x) * part, part), :] = a_got[...]
        halves[pl.ds(base + (2 + y) * part, part), :] = b_own[...]
        halves[pl.ds(base + (3 - y) * part, part), :] = b_got[...]
    feat = own_rows.shape[1]
    blocks = feat // EDGE
    half_blocks = blocks // 2
    places = packed_places(blocks)
    row = lax.broadcasted_iota(jnp.int32, (EDGE, EDGE), 0)
    column = lax.broadcasted_iota(jnp.int32, (EDGE, EDGE), 1)
    lane = lax.broadcasted_iota(jnp.int32, (1, EDGE), 1)
    scale = 1.0 / row_total
    for side in range(2):

        @pl.when(core == side)
        def _():
            start = {}
            for owner in range(2):
                base = 0 if owner == side else 4 * part
                for i, j, first in places[owner]:
                    start[i, j] = base + first
            across, down = [], []
            for i in range(blocks):
                tail = halves[pl.ds(start[i, i] + EDGE - 8, 8), :]
                turned = pltpu.roll(tail, EDGE // 2, 1)
                average = jnp.where(lane < EDGE // 2, tail[7:8], turned[6:7]) * scale
                average_out[:, i * EDGE : (i + 1) * EDGE] = average
                wide = jnp.broadcast_to(average, (EDGE, EDGE))
                across.append(average)
                down.append(jnp.transpose(wide))
            squares = jnp.zeros((EDGE, EDGE), F32)

            def put(i, j, block):
                p, q = (i + half_blocks * side) % blocks, (j + half_blocks * side) % blocks
                centred[pl.ds(p * EDGE, EDGE), pl.ds(q * EDGE, EDGE)] = block

            for i in range(blocks):
                for j in range(i, blocks):
                    block = halves[pl.ds(start[i, j], EDGE), :] * scale - down[i] * across[j]
                    if i == j:
                        block = jnp.where(column >= row, block, jnp.transpose(block))
                        block = block + jnp.where(row == column, COV_EPS, 0.0)
                        squares = squares + block * block
                        put(i, i, block)
                    else:
                        squares = squares + 2.0 * (block * block)
                        put(i, j, block)
                        put(j, i, jnp.transpose(block))
            norm = jnp.sqrt(jnp.sum(jnp.sum(squares, axis=0, keepdims=True), axis=1, keepdims=True))
            factor = 1.0 / norm
            middle = feat // 2
            own = centred[:middle, :] * factor
            own_rows[...] = own
            split_into(own, own_pair)
            theirs = jnp.concatenate([centred[middle:, middle:], centred[middle:, :middle]], axis=1)
            split_into(theirs * factor, other_pair)


def two(value):
    high = value.astype(BF16)
    return high, (value - high.astype(F32)).astype(BF16)


def split_into(value, pair_refs):
    high, low = two(value)
    both = jnp.concatenate([high, low], axis=0)
    rows = both.shape[0] // len(pair_refs)
    for k, ref in enumerate(pair_refs):
        ref[...] = both[k * rows : (k + 1) * rows, :]


def load_full(own_refs, other_refs, high_ref, low_ref):
    middle = high_ref.shape[0] // 2
    rows = own_refs[0].shape[0]
    for k, (own_ref, other_ref) in enumerate(zip(own_refs, other_refs)):
        full = high_ref if k * rows < middle else low_ref
        first = k * rows % middle
        mine = pl.ds(first, rows)
        theirs = pl.ds(middle + first, rows)
        full[mine, :] = own_ref[...]
        full[theirs, :middle] = other_ref[:, middle:]
        full[theirs, middle:] = other_ref[:, :middle]


def times(high, low, high_ref, low_ref):
    return (
        jnp.dot(high, high_ref[...], preferred_element_type=F32)
        + jnp.dot(high, low_ref[...], preferred_element_type=F32)
        + jnp.dot(low, high_ref[...], preferred_element_type=F32)
    )


def power_kernel(own_ref, *refs):
    pair, other = refs[:CUTS], refs[CUTS : 2 * CUTS]
    out_ref, *out_pair, high, low = refs[-CUTS - 3 :]
    load_full(pair, other, high, low)
    middle = own_ref.shape[0]
    square = times(high[:middle, :], low[:middle, :], high, low)
    cube = times(*two(square), high, low)
    result = 2.25 * own_ref[...] - 1.5 * square + 0.25 * cube
    out_ref[...] = result
    split_into(result, out_pair)


def root_kernel(factor, first, last, own_ref, root_ref, *refs):
    pair, other = refs[:CUTS], refs[CUTS : 2 * CUTS]
    out_ref, high, low = refs[-3:]
    load_full(pair, other, high, low)
    root = root_ref[...] * -0.5 if first else root_ref[...]
    result = 1.5 * root - 0.5 * factor * own_ref[...] - 0.5 * times(*two(root), high, low)
    if last:
        row = lax.broadcasted_iota(jnp.int32, result.shape, 0)
        column = lax.broadcasted_iota(jnp.int32, result.shape, 1)
        result = (result + jnp.where(row == column, 1.5 * factor, 0.0)).astype(BF16)
    out_ref[...] = result


def whiten_rows(rows, root_ref, offset):
    projected = jnp.dot(rows, root_ref[...], preferred_element_type=F32) - offset
    energy = jnp.sum(projected * projected, axis=1, keepdims=True)
    return (projected * lax.rsqrt(energy + UNIT_EPS)).astype(BF16)


def build_root(own_root, other_root, average_ref, root, offset_ref):
    core = core_bit()
    middle, feat = own_root.shape
    root[pl.ds(core * middle, middle), :] = own_root[...]
    theirs = pl.ds((1 - core) * middle, middle)
    root[theirs, : feat // 2] = other_root[:, feat // 2 :]
    root[theirs, feat // 2 :] = other_root[:, : feat // 2]
    average = jnp.broadcast_to(average_ref[...], (16, feat))
    high, low = two(average)
    lowest = (average - high.astype(F32) - low.astype(F32)).astype(BF16)
    offset_ref[...] = (
        jnp.dot(high, root[...], preferred_element_type=F32)
        + jnp.dot(low, root[...], preferred_element_type=F32)
        + jnp.dot(lowest, root[...], preferred_element_type=F32)
    )[0:1]


def similarity(own_units, units):
    return lax.dot_general(
        own_units, units, (((1,), (1,)), ((), ())), preferred_element_type=F32
    )


def column_ids(ids):
    return jnp.transpose(jnp.broadcast_to(ids, (ids.shape[1], ids.shape[1])))


def off_diagonal(rows):
    row = lax.broadcasted_iota(jnp.int32, (rows, rows), 0)
    return row != lax.broadcasted_iota(jnp.int32, (rows, rows), 1)


def highest(best):
    return jnp.max(jnp.transpose(best), axis=0, keepdims=True)


def score_column_kernel(
    length, own_root, other_root, average_ref, ids_ref, values_ref, beside_ref, *refs
):
    column, (out_ref, beside_out, root, offset_ref) = refs[:-4], refs[-4:]
    me = lax.axis_index("grp")
    build_root(own_root, other_root, average_ref, root, offset_ref)
    offset = offset_ref[...]
    own = whiten_rows(values_ref[...], root, offset)
    beside = whiten_rows(beside_ref[...], root, offset)
    own_ids, beside_ids = column_ids(ids_ref[0:1, :]), column_ids(ids_ref[1:2, :])
    best = beside_best = None
    for t in range(length):
        units = whiten_rows(column[t - 1][...], root, offset) if t else own
        source = (z_pos() + t) % length * 2 + x_bit()
        ids = ids_ref[pl.ds(source ^ me, 1), :]
        same = own_ids == ids
        if t == 0:
            same = same & off_diagonal(values_ref.shape[0])
        found = jnp.where(same, similarity(own, units), -1.0)
        beside_found = jnp.where(beside_ids == ids, similarity(beside, units), -1.0)
        best = jnp.maximum(best, found) if t else found
        beside_best = jnp.maximum(beside_best, beside_found) if t else beside_found
    out_ref[...] = highest(best)
    beside_out[...] = highest(beside_best)


def larger_kernel(first_ref, second_ref, out_ref):
    out_ref[...] = jnp.maximum(first_ref[...], second_ref[...])


def score_kernel(
    own_root, other_root, average_ref, ids_ref, values_ref, piece_ref,
    out_ref, root, offset_ref, own_units, best,
):
    step = pl.program_id(0)
    me = lax.axis_index("grp")

    @pl.when(step == 0)
    def _():
        build_root(own_root, other_root, average_ref, root, offset_ref)
        own_units[...] = whiten_rows(values_ref[...], root, offset_ref[...])
        best[...] = jnp.full(best.shape, -1.0, F32)

    units = whiten_rows(piece_ref[...], root, offset_ref[...])
    same = column_ids(ids_ref[0:1, :]) == ids_ref[pl.ds(step ^ me, 1), :]
    same = same & (off_diagonal(values_ref.shape[0]) | (step != me))
    best[...] = jnp.maximum(best[...], jnp.where(same, similarity(own_units[...], units), -1.0))

    @pl.when(step == pl.num_programs(0) - 1)
    def _():
        out_ref[...] = highest(best[...])


def pick_kernel(limit, near_ref, far_ref, out_ref):
    z = z_pos()

    def put(ref):
        out_ref[...] = ref[...]

    pl.when(z < limit)(lambda: put(near_ref))
    pl.when(z >= limit)(lambda: put(far_ref))


def hold_kernel(source_ref, *refs):
    refs[-1][...] = source_ref[...]


def hold(array, after):
    return call(
        hold_kernel, [jax.ShapeDtypeStruct(array.shape, array.dtype)], [array], after=after
    )[0]


def join_kernel(first_ref, second_ref, out_ref):
    rows = first_ref.shape[0]
    out_ref[:rows, :] = first_ref[...]
    out_ref[rows:, :] = second_ref[...]


class Ids:
    def __init__(self, cluster):
        self.size = lax.axis_size("grp")
        self.held = cluster.reshape(1, cluster.shape[0])

    def step(self):
        count, columns = self.held.shape
        if count < self.size:
            got = swap(self.held, "grp", count)
            (self.held,) = call(
                join_kernel, [shape(2 * count, columns, jnp.int32)], [self.held, got]
            )
        return [self.held]

    def all(self):
        while self.held.shape[0] < self.size:
            self.step()
        return self.held


class Gather:
    def __init__(self, values):
        self.length = lax.axis_size("grp") // 2
        self.values = values
        self.right, self.left = {0: values}, {0: values}

    def along(self, t, after=()):
        size, length = 2 * self.length, self.length
        right, left = self.right[t - 1], self.left[t - 1]
        if after:
            right, left = hold(right, after), hold(left, after)
        to_left = [(g, g - 2) for g in range(size) if 1 <= g // 2 <= length - t]
        to_right = [(g, g + 2) for g in range(size) if t - 1 <= g // 2 <= length - 2]
        self.right[t] = lax.ppermute(right, "grp", to_left)
        self.left[t] = lax.ppermute(left, "grp", to_right)
        return [self.right[t], self.left[t]]

    def across(self, after=()):
        self.beside = swap(hold(self.values, after) if after else self.values, "grp", 1)
        return [self.beside]

    def column(self):
        pieces = []
        for t in range(1, self.length):
            kernel = functools.partial(pick_kernel, self.length - t)
            both = [self.right[t], self.left[self.length - t]]
            pieces += call(kernel, [shape(*self.values.shape, BF16)], both)
        return pieces


def best_cosines(own_root, other_root, average, ids, values, gathered):
    rows, feat = values.shape
    group = lax.axis_size("grp")
    scratch = [pltpu.VMEM((feat, feat), BF16), pltpu.VMEM((1, feat), F32)]
    flops = 2 * group * rows * feat * (feat + rows)
    ins = [own_root, other_root, average, ids, values]
    if isinstance(gathered, Gather):
        kernel = functools.partial(score_column_kernel, gathered.length)
        ins += [gathered.beside] + gathered.column()
        both = [shape(1, rows)] * 2
        best, beside = call(kernel, both, ins, flops, scratch, SCORE_BYTES)
        return call(larger_kernel, [shape(1, rows)], [best, swap(beside, "grp", 1)])[0]
    full = lambda array: pl.BlockSpec(array.shape, lambda i: (0, 0))
    return pl.pallas_call(
        score_kernel,
        grid=(group,),
        out_shape=shape(1, rows),
        in_specs=[full(array) for array in ins] + [pl.BlockSpec((rows, feat), lambda i: (i, 0))],
        out_specs=pl.BlockSpec((1, rows), lambda i: (0, 0)),
        scratch_shapes=scratch + [pltpu.VMEM((rows, feat), BF16), pltpu.VMEM((rows, rows), F32)],
        compiler_params=pltpu.CompilerParams(vmem_limit_bytes=SCORE_BYTES),
        cost_estimate=pl.CostEstimate(
            flops=flops, bytes_accessed=2 * group * rows * feat, transcendentals=0
        ),
    )(*ins, gathered)


def reduce_gram(values, blocks, gather, ids):
    length = lax.axis_size("grp") // 2
    part = -(-EDGE * (blocks * (blocks + 1) // 2) // (16 * length * 8)) * 8
    rows = part * length * 8
    swapped = swap(values, "rep", 1)
    a_keep, a_send, b_keep, b_send = call(
        gram_kernel,
        [shape(rows // 4, EDGE)] * 4,
        [values, swapped],
        flops=values.shape[0] * 2 * rows * EDGE * 2,
        scratch=[pltpu.VMEM((rows, EDGE), F32)],
    )
    a_got, b_got = swap(a_send, "grp", 1), swap(b_send, "rep", 2)
    second = [shape(rows // 8, EDGE)] * 2
    wait = ids.step()
    a_keep, a_send = call(functools.partial(halve_kernel, y_bit), second, [a_keep, a_got], after=wait)
    b_keep, b_send = call(functools.partial(halve_kernel, x_bit), second, [b_keep, b_got], after=wait)
    wait = ids.step()
    a_got, b_got = swap(a_send, "rep", 2), swap(b_send, "grp", 1)
    pieces = call(
        functools.partial(line_split_kernel, length),
        [shape(2 * part, EDGE)] * length,
        [a_keep, a_got, b_keep, b_got],
        after=wait + (gather.along(1) if gather else []),
    )
    got = [swap(pieces[d], "grp", 2 * d) for d in range(1, length)]
    (total,) = call(line_sum_kernel, [shape(2 * part, EDGE)], [pieces[0]] + got)
    got = [swap(total, "grp", 2 * d) for d in range(1, length)]
    wait = ids.step()
    if gather:
        wait = wait + gather.across([pieces[0]])
    a_own, b_own = call(
        functools.partial(line_join_kernel, length), second, [total] + got, after=wait
    )
    wait = gather.along(2, [a_own]) if gather else []
    a_got, b_got = swap(a_own, "rep", 2), swap(b_own, "grp", 1)
    third = [shape(rows // 4, EDGE)]
    (a_own,) = call(functools.partial(pair_join_kernel, y_bit), third, [a_own, a_got])
    (b_own,) = call(functools.partial(pair_join_kernel, x_bit), third, [b_own, b_got])
    a_got, b_got = swap(a_own, "grp", 1), swap(b_own, "rep", 2)
    own = [a_own, a_got, b_own, b_got]
    return own + [swap(piece, "rep", 1) for piece in own], wait


def inverse_root_slabs(own, pair, other, feat, gather, after):
    middle = feat // 2
    full = [pltpu.VMEM((feat, feat), BF16)] * 2
    flops = 2 * 3 * middle * feat * feat
    outs = [shape(middle, feat)] + [shape(2 * middle // CUTS, feat, BF16)] * CUTS
    root, factor = own, 1.5
    waits = {2: gather.along(3, [own])} if gather else {}
    for step in range(STEPS):
        last = step == STEPS - 1
        if not last:
            power, *power_pair = call(
                power_kernel, outs, [own] + pair + other, 2 * flops, full, NEWTON_BYTES, after
            )
            power_other = [swap(piece, "rep", 1) for piece in power_pair]
        if step > 0:
            (root,) = call(
                functools.partial(root_kernel, factor, step == 1, last),
                [shape(middle, feat, BF16 if last else F32)],
                [own, root] + pair + other,
                flops,
                full,
                NEWTON_BYTES,
                waits.get(step, ()),
            )
            factor, after = 1.5 * factor, [root]
        if not last:
            own, pair, other = power, power_pair, power_other
    return root, swap(root, "rep", 1)


def local(embeddings, scales, cluster, cluster_rank):
    row_count, feat = embeddings.shape
    group = lax.axis_size("grp")
    row_total = row_count * group * lax.axis_size("rep")
    (values,) = call(dequantize_kernel, [shape(row_count, feat, BF16)], [embeddings, scales])
    ids = Ids(cluster)
    gather, gathered = None, None
    if group * values.size * values.dtype.itemsize <= IN_PIECES_BYTES:
        gather = Gather(values)
    else:
        gathered = lax.all_gather(values, "grp", axis=0, tiled=True)
    pieces, wait = reduce_gram(values, feat // EDGE, gather, ids)
    middle = feat // 2
    pair_shapes = [shape(2 * middle // CUTS, feat, BF16)] * (2 * CUTS)
    own, average, *pairs = call(
        functools.partial(unpack_kernel, row_total),
        [shape(middle, feat), shape(1, feat)] + pair_shapes,
        pieces,
        scratch=[pltpu.VMEM((8 * pieces[0].shape[0], EDGE), F32), pltpu.VMEM((feat, feat), F32)],
        limit=UNPACK_BYTES,
    )
    own_root, other_root = inverse_root_slabs(own, pairs[:CUTS], pairs[CUTS:], feat, gather, wait)
    best = best_cosines(own_root, other_root, average, ids.all(), values, gather or gathered)
    return best.reshape(row_count)


def solution(mesh):
    placed = (
        P(("grp", "rep"), None),
        P(("grp", "rep"), None),
        P(("grp", "rep")),
        P(("grp", "rep")),
    )
    return jax.shard_map(
        local, mesh=mesh, in_specs=placed, out_specs=P(("grp", "rep")), check_vma=False
    )
```

```python
import functools

import jax
import jax.numpy as jnp
from jax import lax
from jax.experimental import pallas as pl
from jax.experimental.pallas import tpu as pltpu
from jax.sharding import PartitionSpec as P

STEPS = 5
COV_EPS = 0.001
UNIT_EPS = 1e-06
EDGE = 128
F32 = jnp.float32
BF16 = jnp.bfloat16
SMALL_BYTES = 6 * 2**20
UNPACK_BYTES = 14 * 2**20
NEWTON_BYTES = 14 * 2**20
SCORE_BYTES = 16 * 2**20
IN_PIECES_BYTES = 8 * 2**20
CUTS = 4
EXACT_FROM = 3


def swap(array, axis, bit):
    size = lax.axis_size(axis)
    return lax.ppermute(array, axis, [(i, i ^ bit) for i in range(size)])


def whole(count):
    return [pl.BlockSpec(memory_space=pltpu.VMEM)] * count


def call(kernel, outs, ins, flops=0, scratch=(), limit=SMALL_BYTES, after=()):
    moved = sum(a.size * a.dtype.itemsize for a in list(ins) + list(outs))
    return pl.pallas_call(
        kernel,
        out_shape=outs,
        in_specs=whole(len(ins)) + [pl.BlockSpec(memory_space=pl.ANY)] * len(after),
        out_specs=whole(len(outs)),
        scratch_shapes=list(scratch),
        compiler_params=pltpu.CompilerParams(vmem_limit_bytes=limit),
        cost_estimate=pl.CostEstimate(flops=flops, bytes_accessed=moved, transcendentals=0),
    )(*ins, *after)


def shape(rows, columns, dtype=F32):
    return jax.ShapeDtypeStruct((rows, columns), dtype)


def core_bit():
    return lax.axis_index("rep") % 2


def y_bit():
    return lax.axis_index("rep") // 2


def x_bit():
    return lax.axis_index("grp") % 2


def z_pos():
    return lax.axis_index("grp") // 2


def block_rows(blocks):
    total = blocks * (blocks + 1) // 2
    halves, room = ([], []), total // 2
    for i in range(blocks):
        if blocks - i <= room:
            halves[0].append(i)
            room -= blocks - i
        else:
            halves[1].append(i)
    return halves


def packed_places(blocks):
    places = []
    for rows in block_rows(blocks):
        pairs = [(i, j) for i in rows for j in range(i, blocks)]
        places.append([(i, j, EDGE * k) for k, (i, j) in enumerate(pairs)])
    return places


def dequantize_kernel(emb_ref, scale_ref, out_ref):
    blocks = scale_ref.shape[1]
    width = emb_ref.shape[1] // blocks
    for b in range(blocks):
        columns = pl.ds(b * width, width)
        out_ref[:, columns] = (
            emb_ref[:, columns].astype(F32) * scale_ref[:, b : b + 1]
        ).astype(BF16)


def gram_kernel(own_ref, other_ref, a_keep, a_send, b_keep, b_send, packed):
    blocks = own_ref.shape[1] // EDGE
    contract = (((0,), (0,)), ((), ()))
    core, x, y = core_bit(), x_bit(), y_bit()
    row = lax.broadcasted_iota(jnp.int32, (EDGE, EDGE), 0)
    column = lax.broadcasted_iota(jnp.int32, (EDGE, EDGE), 1)
    half = EDGE // 2
    places = packed_places(blocks)
    if packed.shape[0] > EDGE * len(places[0]):
        packed[...] = jnp.zeros_like(packed)
    for side in range(2):

        @pl.when(core == side)
        def _():
            first = {(i, j): start for i, j, start in places[side]}
            for i in block_rows(blocks)[side]:
                mine = pl.ds(i * EDGE, EDGE)
                rest = pl.ds(i * EDGE, (blocks - i) * EDGE)
                total = lax.dot_general(
                    own_ref[:, mine], own_ref[:, rest], contract, preferred_element_type=F32
                ) + lax.dot_general(
                    other_ref[:, mine], other_ref[:, rest], contract, preferred_element_type=F32
                )
                sums = jnp.sum(own_ref[:, mine].astype(F32), axis=0, keepdims=True) + jnp.sum(
                    other_ref[:, mine].astype(F32), axis=0, keepdims=True
                )
                turned = pltpu.roll(jnp.broadcast_to(sums, (8, EDGE)), half, 1)[0:1]
                diagonal = total[:, :EDGE]
                diagonal = jnp.where((row == EDGE - 1) & (column < half), sums, diagonal)
                diagonal = jnp.where((row == EDGE - 2) & (column < half), turned, diagonal)
                packed[pl.ds(first[i, i], EDGE), :] = diagonal
                for j in range(i + 1, blocks):
                    packed[pl.ds(first[i, j], EDGE), :] = total[
                        :, (j - i) * EDGE : (j - i + 1) * EDGE
                    ]

    part = a_keep.shape[0]
    a_keep[...] = packed[pl.ds(x * part, part), :]
    a_send[...] = packed[pl.ds((1 - x) * part, part), :]
    b_keep[...] = packed[pl.ds((2 + y) * part, part), :]
    b_send[...] = packed[pl.ds((3 - y) * part, part), :]


def halve_kernel(which, keep_ref, got_ref, *refs):
    keep_out, send_out = refs[-2:]
    bit = which()
    part = keep_out.shape[0]
    mine, theirs = pl.ds(bit * part, part), pl.ds((1 - bit) * part, part)
    keep_out[...] = keep_ref[mine, :] + got_ref[mine, :]
    send_out[...] = keep_ref[theirs, :] + got_ref[theirs, :]


def line_split_kernel(length, a_keep, a_got, b_keep, b_got, *refs):
    outs = refs[-length:]
    z = z_pos()
    part = a_keep.shape[0] // length
    for d in range(length):
        rows = pl.ds((z ^ d) * part, part)
        outs[d][:part, :] = a_keep[rows, :] + a_got[rows, :]
        outs[d][part:, :] = b_keep[rows, :] + b_got[rows, :]


def line_sum_kernel(*refs):
    total = refs[0][...]
    for ref in refs[1:-1]:
        total = total + ref[...]
    refs[-1][...] = total


def line_join_kernel(length, *refs):
    z = z_pos()
    a_out, b_out = refs[-2:]
    part = a_out.shape[0] // length
    for d in range(length):
        rows = pl.ds((z ^ d) * part, part)
        a_out[rows, :] = refs[d][:part, :]
        b_out[rows, :] = refs[d][part:, :]


def pair_join_kernel(which, own_ref, got_ref, out_ref):
    bit = which()
    part = own_ref.shape[0]
    out_ref[pl.ds(bit * part, part), :] = own_ref[...]
    out_ref[pl.ds((1 - bit) * part, part), :] = got_ref[...]


def unpack_kernel(row_total, *refs):
    own_rows, average_out, *pairs, halves, centred = refs[-2 * CUTS - 4 :]
    own_pair, other_pair = pairs[:CUTS], pairs[CUTS:]
    core, x, y = core_bit(), x_bit(), y_bit()
    part = refs[0].shape[0]
    for h in range(2):
        base = 4 * part * h
        a_own, a_got, b_own, b_got = refs[4 * h : 4 * h + 4]
        halves[pl.ds(base + x * part, part), :] = a_own[...]
        halves[pl.ds(base + (1 - x) * part, part), :] = a_got[...]
        halves[pl.ds(base + (2 + y) * part, part), :] = b_own[...]
        halves[pl.ds(base + (3 - y) * part, part), :] = b_got[...]
    feat = own_rows.shape[1]
    blocks = feat // EDGE
    half_blocks = blocks // 2
    places = packed_places(blocks)
    row = lax.broadcasted_iota(jnp.int32, (EDGE, EDGE), 0)
    column = lax.broadcasted_iota(jnp.int32, (EDGE, EDGE), 1)
    lane = lax.broadcasted_iota(jnp.int32, (1, EDGE), 1)
    scale = 1.0 / row_total
    for side in range(2):

        @pl.when(core == side)
        def _():
            start = {}
            for owner in range(2):
                base = 0 if owner == side else 4 * part
                for i, j, first in places[owner]:
                    start[i, j] = base + first
            across, down = [], []
            for i in range(blocks):
                tail = halves[pl.ds(start[i, i] + EDGE - 8, 8), :]
                turned = pltpu.roll(tail, EDGE // 2, 1)
                average = jnp.where(lane < EDGE // 2, tail[7:8], turned[6:7]) * scale
                average_out[:, i * EDGE : (i + 1) * EDGE] = average
                wide = jnp.broadcast_to(average, (EDGE, EDGE))
                across.append(average)
                down.append(jnp.transpose(wide))
            squares = jnp.zeros((EDGE, EDGE), F32)

            def put(i, j, block):
                p, q = (i + half_blocks * side) % blocks, (j + half_blocks * side) % blocks
                centred[pl.ds(p * EDGE, EDGE), pl.ds(q * EDGE, EDGE)] = block

            for i in range(blocks):
                for j in range(i, blocks):
                    block = halves[pl.ds(start[i, j], EDGE), :] * scale - down[i] * across[j]
                    if i == j:
                        block = jnp.where(column >= row, block, jnp.transpose(block))
                        block = block + jnp.where(row == column, COV_EPS, 0.0)
                        squares = squares + block * block
                        put(i, i, block)
                    else:
                        squares = squares + 2.0 * (block * block)
                        put(i, j, block)
                        put(j, i, jnp.transpose(block))
            norm = jnp.sqrt(jnp.sum(jnp.sum(squares, axis=0, keepdims=True), axis=1, keepdims=True))
            factor = 1.0 / norm
            middle = feat // 2
            own = centred[:middle, :] * factor
            own_rows[...] = own
            split_into(own, own_pair)
            theirs = jnp.concatenate([centred[middle:, middle:], centred[middle:, :middle]], axis=1)
            split_into(theirs * factor, other_pair)


def two(value):
    high = value.astype(BF16)
    return high, (value - high.astype(F32)).astype(BF16)


def split_into(value, pair_refs):
    high, low = two(value)
    both = jnp.concatenate([high, low], axis=0)
    rows = both.shape[0] // len(pair_refs)
    for k, ref in enumerate(pair_refs):
        ref[...] = both[k * rows : (k + 1) * rows, :]


def load_full(own_refs, other_refs, high_ref, low_ref):
    middle = high_ref.shape[0] // 2
    rows = own_refs[0].shape[0]
    for k, (own_ref, other_ref) in enumerate(zip(own_refs, other_refs)):
        full = high_ref if k * rows < middle else low_ref
        first = k * rows % middle
        mine = pl.ds(first, rows)
        theirs = pl.ds(middle + first, rows)
        full[mine, :] = own_ref[...]
        full[theirs, :middle] = other_ref[:, middle:]
        full[theirs, middle:] = other_ref[:, :middle]


def times(high, low, high_ref, low_ref):
    return (
        jnp.dot(high, high_ref[...], preferred_element_type=F32)
        + jnp.dot(high, low_ref[...], preferred_element_type=F32)
        + jnp.dot(low, high_ref[...], preferred_element_type=F32)
    )


def power_kernel(exact, own_ref, *refs):
    pair, other = refs[:CUTS], refs[CUTS : 2 * CUTS]
    out_ref, *out_pair, high, low = refs[-CUTS - 3 :]
    load_full(pair, other, high, low)
    middle = own_ref.shape[0]
    square = times(high[:middle, :], low[:middle, :], high, low)
    if exact:
        cube = times(*two(square), high, low)
    else:
        cube = jnp.dot(square.astype(BF16), high[...], preferred_element_type=F32)
    result = 2.25 * own_ref[...] - 1.5 * square + 0.25 * cube
    out_ref[...] = result
    split_into(result, out_pair)


def root_kernel(factor, first, last, own_ref, root_ref, *refs):
    pair, other = refs[:CUTS], refs[CUTS : 2 * CUTS]
    out_ref, high, low = refs[-3:]
    load_full(pair, other, high, low)
    root = root_ref[...] * -0.5 if first else root_ref[...]
    if first:
        product = jnp.dot(root.astype(BF16), high[...], preferred_element_type=F32)
    else:
        product = times(*two(root), high, low)
    result = 1.5 * root - 0.5 * factor * own_ref[...] - 0.5 * product
    if last:
        row = lax.broadcasted_iota(jnp.int32, result.shape, 0)
        column = lax.broadcasted_iota(jnp.int32, result.shape, 1)
        result = (result + jnp.where(row == column, 1.5 * factor, 0.0)).astype(BF16)
    out_ref[...] = result


def whiten_rows(rows, root_ref, offset):
    projected = jnp.dot(rows, root_ref[...], preferred_element_type=F32) - offset
    energy = jnp.sum(projected * projected, axis=1, keepdims=True)
    return (projected * lax.rsqrt(energy + UNIT_EPS)).astype(BF16)


def build_root(own_root, other_root, average_ref, root, offset_ref):
    core = core_bit()
    middle, feat = own_root.shape
    root[pl.ds(core * middle, middle), :] = own_root[...]
    theirs = pl.ds((1 - core) * middle, middle)
    root[theirs, : feat // 2] = other_root[:, feat // 2 :]
    root[theirs, feat // 2 :] = other_root[:, : feat // 2]
    average = jnp.broadcast_to(average_ref[...], (16, feat))
    high, low = two(average)
    lowest = (average - high.astype(F32) - low.astype(F32)).astype(BF16)
    offset_ref[...] = (
        jnp.dot(high, root[...], preferred_element_type=F32)
        + jnp.dot(low, root[...], preferred_element_type=F32)
        + jnp.dot(lowest, root[...], preferred_element_type=F32)
    )[0:1]


def similarity(own_units, units):
    return lax.dot_general(
        own_units, units, (((1,), (1,)), ((), ())), preferred_element_type=F32
    )


def column_ids(ids):
    return jnp.transpose(jnp.broadcast_to(ids, (ids.shape[1], ids.shape[1])))


def off_diagonal(rows):
    row = lax.broadcasted_iota(jnp.int32, (rows, rows), 0)
    return row != lax.broadcasted_iota(jnp.int32, (rows, rows), 1)


def highest(best):
    return jnp.max(jnp.transpose(best), axis=0, keepdims=True)


def score_column_kernel(
    length, own_root, other_root, average_ref, ids_ref, values_ref, beside_ref, *refs
):
    column, (out_ref, beside_out, root, offset_ref) = refs[:-4], refs[-4:]
    me = lax.axis_index("grp")
    build_root(own_root, other_root, average_ref, root, offset_ref)
    offset = offset_ref[...]
    own = whiten_rows(values_ref[...], root, offset)
    beside = whiten_rows(beside_ref[...], root, offset)
    own_ids, beside_ids = column_ids(ids_ref[0:1, :]), column_ids(ids_ref[1:2, :])
    best = beside_best = None
    for t in range(length):
        units = whiten_rows(column[t - 1][...], root, offset) if t else own
        source = (z_pos() + t) % length * 2 + x_bit()
        ids = ids_ref[pl.ds(source ^ me, 1), :]
        same = own_ids == ids
        if t == 0:
            same = same & off_diagonal(values_ref.shape[0])
        found = jnp.where(same, similarity(own, units), -1.0)
        beside_found = jnp.where(beside_ids == ids, similarity(beside, units), -1.0)
        best = jnp.maximum(best, found) if t else found
        beside_best = jnp.maximum(beside_best, beside_found) if t else beside_found
    out_ref[...] = highest(best)
    beside_out[...] = highest(beside_best)


def larger_kernel(first_ref, second_ref, out_ref):
    out_ref[...] = jnp.maximum(first_ref[...], second_ref[...])


def score_kernel(
    own_root, other_root, average_ref, ids_ref, values_ref, piece_ref,
    out_ref, root, offset_ref, own_units, best,
):
    step = pl.program_id(0)
    me = lax.axis_index("grp")

    @pl.when(step == 0)
    def _():
        build_root(own_root, other_root, average_ref, root, offset_ref)
        own_units[...] = whiten_rows(values_ref[...], root, offset_ref[...])
        best[...] = jnp.full(best.shape, -1.0, F32)

    units = whiten_rows(piece_ref[...], root, offset_ref[...])
    same = column_ids(ids_ref[0:1, :]) == ids_ref[pl.ds(step ^ me, 1), :]
    same = same & (off_diagonal(values_ref.shape[0]) | (step != me))
    best[...] = jnp.maximum(best[...], jnp.where(same, similarity(own_units[...], units), -1.0))

    @pl.when(step == pl.num_programs(0) - 1)
    def _():
        out_ref[...] = highest(best[...])


def pick_kernel(limit, near_ref, far_ref, out_ref):
    z = z_pos()

    def put(ref):
        out_ref[...] = ref[...]

    pl.when(z < limit)(lambda: put(near_ref))
    pl.when(z >= limit)(lambda: put(far_ref))


def hold_kernel(source_ref, *refs):
    refs[-1][...] = source_ref[...]


def hold(array, after):
    return call(
        hold_kernel, [jax.ShapeDtypeStruct(array.shape, array.dtype)], [array], after=after
    )[0]


def join_kernel(first_ref, second_ref, out_ref):
    rows = first_ref.shape[0]
    out_ref[:rows, :] = first_ref[...]
    out_ref[rows:, :] = second_ref[...]


class Ids:
    def __init__(self, cluster):
        self.size = lax.axis_size("grp")
        self.held = cluster.reshape(1, cluster.shape[0])

    def step(self):
        count, columns = self.held.shape
        if count < self.size:
            got = swap(self.held, "grp", count)
            (self.held,) = call(
                join_kernel, [shape(2 * count, columns, jnp.int32)], [self.held, got]
            )
        return [self.held]

    def all(self):
        while self.held.shape[0] < self.size:
            self.step()
        return self.held


class Gather:
    def __init__(self, values):
        self.length = lax.axis_size("grp") // 2
        self.values = values
        self.right, self.left = {0: values}, {0: values}

    def along(self, t, after=()):
        size, length = 2 * self.length, self.length
        right, left = self.right[t - 1], self.left[t - 1]
        if after:
            right, left = hold(right, after), hold(left, after)
        to_left = [(g, g - 2) for g in range(size) if 1 <= g // 2 <= length - t]
        to_right = [(g, g + 2) for g in range(size) if t - 1 <= g // 2 <= length - 2]
        self.right[t] = lax.ppermute(right, "grp", to_left)
        self.left[t] = lax.ppermute(left, "grp", to_right)
        return [self.right[t], self.left[t]]

    def across(self, after=()):
        self.beside = swap(hold(self.values, after) if after else self.values, "grp", 1)
        return [self.beside]

    def column(self):
        pieces = []
        for t in range(1, self.length):
            kernel = functools.partial(pick_kernel, self.length - t)
            both = [self.right[t], self.left[self.length - t]]
            pieces += call(kernel, [shape(*self.values.shape, BF16)], both)
        return pieces


def best_cosines(own_root, other_root, average, ids, values, gathered):
    rows, feat = values.shape
    group = lax.axis_size("grp")
    scratch = [pltpu.VMEM((feat, feat), BF16), pltpu.VMEM((1, feat), F32)]
    flops = 2 * group * rows * feat * (feat + rows)
    ins = [own_root, other_root, average, ids, values]
    if isinstance(gathered, Gather):
        kernel = functools.partial(score_column_kernel, gathered.length)
        ins += [gathered.beside] + gathered.column()
        both = [shape(1, rows)] * 2
        best, beside = call(kernel, both, ins, flops, scratch, SCORE_BYTES)
        return call(larger_kernel, [shape(1, rows)], [best, swap(beside, "grp", 1)])[0]
    full = lambda array: pl.BlockSpec(array.shape, lambda i: (0, 0))
    return pl.pallas_call(
        score_kernel,
        grid=(group,),
        out_shape=shape(1, rows),
        in_specs=[full(array) for array in ins] + [pl.BlockSpec((rows, feat), lambda i: (i, 0))],
        out_specs=pl.BlockSpec((1, rows), lambda i: (0, 0)),
        scratch_shapes=scratch + [pltpu.VMEM((rows, feat), BF16), pltpu.VMEM((rows, rows), F32)],
        compiler_params=pltpu.CompilerParams(vmem_limit_bytes=SCORE_BYTES),
        cost_estimate=pl.CostEstimate(
            flops=flops, bytes_accessed=2 * group * rows * feat, transcendentals=0
        ),
    )(*ins, gathered)


def reduce_gram(values, blocks, gather, ids):
    length = lax.axis_size("grp") // 2
    part = -(-EDGE * (blocks * (blocks + 1) // 2) // (16 * length * 8)) * 8
    rows = part * length * 8
    swapped = swap(values, "rep", 1)
    a_keep, a_send, b_keep, b_send = call(
        gram_kernel,
        [shape(rows // 4, EDGE)] * 4,
        [values, swapped],
        flops=values.shape[0] * 2 * rows * EDGE * 2,
        scratch=[pltpu.VMEM((rows, EDGE), F32)],
    )
    a_got, b_got = swap(a_send, "grp", 1), swap(b_send, "rep", 2)
    second = [shape(rows // 8, EDGE)] * 2
    wait = ids.step()
    a_keep, a_send = call(functools.partial(halve_kernel, y_bit), second, [a_keep, a_got], after=wait)
    b_keep, b_send = call(functools.partial(halve_kernel, x_bit), second, [b_keep, b_got], after=wait)
    wait = ids.step()
    a_got, b_got = swap(a_send, "rep", 2), swap(b_send, "grp", 1)
    pieces = call(
        functools.partial(line_split_kernel, length),
        [shape(2 * part, EDGE)] * length,
        [a_keep, a_got, b_keep, b_got],
        after=wait + (gather.along(1) if gather else []),
    )
    got = [swap(pieces[d], "grp", 2 * d) for d in range(1, length)]
    (total,) = call(line_sum_kernel, [shape(2 * part, EDGE)], [pieces[0]] + got)
    got = [swap(total, "grp", 2 * d) for d in range(1, length)]
    wait = ids.step()
    if gather:
        wait = wait + gather.across([pieces[0]])
    a_own, b_own = call(
        functools.partial(line_join_kernel, length), second, [total] + got, after=wait
    )
    wait = gather.along(2, [a_own]) if gather else []
    a_got, b_got = swap(a_own, "rep", 2), swap(b_own, "grp", 1)
    third = [shape(rows // 4, EDGE)]
    (a_own,) = call(functools.partial(pair_join_kernel, y_bit), third, [a_own, a_got])
    (b_own,) = call(functools.partial(pair_join_kernel, x_bit), third, [b_own, b_got])
    a_got, b_got = swap(a_own, "grp", 1), swap(b_own, "rep", 2)
    own = [a_own, a_got, b_own, b_got]
    return own + [swap(piece, "rep", 1) for piece in own], wait


def inverse_root_slabs(own, pair, other, feat, gather, after):
    middle = feat // 2
    full = [pltpu.VMEM((feat, feat), BF16)] * 2
    flops = 2 * 3 * middle * feat * feat
    outs = [shape(middle, feat)] + [shape(2 * middle // CUTS, feat, BF16)] * CUTS
    root, factor = own, 1.5
    waits = {4: gather.along(3, [own])} if gather else {}
    for step in range(STEPS):
        last = step == STEPS - 1
        if not last:
            power, *power_pair = call(
                functools.partial(power_kernel, step >= EXACT_FROM), outs, [own] + pair + other, 2 * flops, full, NEWTON_BYTES, after
            )
            power_other = [swap(piece, "rep", 1) for piece in power_pair]
        if step > 0:
            (root,) = call(
                functools.partial(root_kernel, factor, step == 1, last),
                [shape(middle, feat, BF16 if last else F32)],
                [own, root] + pair + other,
                flops,
                full,
                NEWTON_BYTES,
                waits.get(step, ()),
            )
            factor, after = 1.5 * factor, [root]
        if not last:
            own, pair, other = power, power_pair, power_other
    return root, swap(root, "rep", 1)


def local(embeddings, scales, cluster, cluster_rank):
    row_count, feat = embeddings.shape
    group = lax.axis_size("grp")
    row_total = row_count * group * lax.axis_size("rep")
    (values,) = call(dequantize_kernel, [shape(row_count, feat, BF16)], [embeddings, scales])
    ids = Ids(cluster)
    gather, gathered = None, None
    if group * values.size * values.dtype.itemsize <= IN_PIECES_BYTES:
        gather = Gather(values)
    else:
        gathered = lax.all_gather(values, "grp", axis=0, tiled=True)
    pieces, wait = reduce_gram(values, feat // EDGE, gather, ids)
    middle = feat // 2
    pair_shapes = [shape(2 * middle // CUTS, feat, BF16)] * (2 * CUTS)
    own, average, *pairs = call(
        functools.partial(unpack_kernel, row_total),
        [shape(middle, feat), shape(1, feat)] + pair_shapes,
        pieces,
        scratch=[pltpu.VMEM((8 * pieces[0].shape[0], EDGE), F32), pltpu.VMEM((feat, feat), F32)],
        limit=UNPACK_BYTES,
    )
    own_root, other_root = inverse_root_slabs(own, pairs[:CUTS], pairs[CUTS:], feat, gather, wait)
    best = best_cosines(own_root, other_root, average, ids.all(), values, gather or gathered)
    return best.reshape(row_count)


def solution(mesh):
    placed = (
        P(("grp", "rep"), None),
        P(("grp", "rep"), None),
        P(("grp", "rep")),
        P(("grp", "rep")),
    )
    return jax.shard_map(
        local, mesh=mesh, in_specs=placed, out_specs=P(("grp", "rep")), check_vma=False
    )
```

```python
import functools

import jax
import jax.numpy as jnp
from jax import lax
from jax.experimental import pallas as pl
from jax.experimental.pallas import tpu as pltpu
from jax.sharding import PartitionSpec as P

STEPS = 5
COV_EPS = 0.001
UNIT_EPS = 1e-06
EDGE = 128
F32 = jnp.float32
BF16 = jnp.bfloat16
SMALL_BYTES = 6 * 2**20
UNPACK_BYTES = 14 * 2**20
NEWTON_BYTES = 14 * 2**20
SCORE_BYTES = 16 * 2**20
IN_PIECES_BYTES = 8 * 2**20
CUTS = 4
EXACT_FROM = 3


def swap(array, axis, bit):
    size = lax.axis_size(axis)
    return lax.ppermute(array, axis, [(i, i ^ bit) for i in range(size)])


def whole(count):
    return [pl.BlockSpec(memory_space=pltpu.VMEM)] * count


def call(kernel, outs, ins, flops=0, scratch=(), limit=SMALL_BYTES, after=()):
    moved = sum(a.size * a.dtype.itemsize for a in list(ins) + list(outs))
    return pl.pallas_call(
        kernel,
        out_shape=outs,
        in_specs=whole(len(ins)) + [pl.BlockSpec(memory_space=pl.ANY)] * len(after),
        out_specs=whole(len(outs)),
        scratch_shapes=list(scratch),
        compiler_params=pltpu.CompilerParams(vmem_limit_bytes=limit),
        cost_estimate=pl.CostEstimate(flops=flops, bytes_accessed=moved, transcendentals=0),
    )(*ins, *after)


def shape(rows, columns, dtype=F32):
    return jax.ShapeDtypeStruct((rows, columns), dtype)


def core_bit():
    return lax.axis_index("rep") % 2


def y_bit():
    return lax.axis_index("rep") // 2


def x_bit():
    return lax.axis_index("grp") % 2


def z_pos():
    return lax.axis_index("grp") // 2


def block_rows(blocks):
    total = blocks * (blocks + 1) // 2
    halves, room = ([], []), total // 2
    for i in range(blocks):
        if blocks - i <= room:
            halves[0].append(i)
            room -= blocks - i
        else:
            halves[1].append(i)
    return halves


def packed_places(blocks):
    places = []
    for rows in block_rows(blocks):
        pairs = [(i, j) for i in rows for j in range(i, blocks)]
        places.append([(i, j, EDGE * k) for k, (i, j) in enumerate(pairs)])
    return places


def dequantize_kernel(emb_ref, scale_ref, out_ref):
    blocks = scale_ref.shape[1]
    width = emb_ref.shape[1] // blocks
    for b in range(blocks):
        columns = pl.ds(b * width, width)
        out_ref[:, columns] = (
            emb_ref[:, columns].astype(F32) * scale_ref[:, b : b + 1]
        ).astype(BF16)


def gram_kernel(own_ref, other_ref, a_keep, a_send, b_keep, b_send, packed):
    blocks = own_ref.shape[1] // EDGE
    contract = (((0,), (0,)), ((), ()))
    core, x, y = core_bit(), x_bit(), y_bit()
    row = lax.broadcasted_iota(jnp.int32, (EDGE, EDGE), 0)
    column = lax.broadcasted_iota(jnp.int32, (EDGE, EDGE), 1)
    half = EDGE // 2
    places = packed_places(blocks)
    if packed.shape[0] > EDGE * len(places[0]):
        packed[...] = jnp.zeros_like(packed)
    for side in range(2):

        @pl.when(core == side)
        def _():
            first = {(i, j): start for i, j, start in places[side]}
            for i in block_rows(blocks)[side]:
                mine = pl.ds(i * EDGE, EDGE)
                rest = pl.ds(i * EDGE, (blocks - i) * EDGE)
                total = lax.dot_general(
                    own_ref[:, mine], own_ref[:, rest], contract, preferred_element_type=F32
                ) + lax.dot_general(
                    other_ref[:, mine], other_ref[:, rest], contract, preferred_element_type=F32
                )
                sums = jnp.sum(own_ref[:, mine].astype(F32), axis=0, keepdims=True) + jnp.sum(
                    other_ref[:, mine].astype(F32), axis=0, keepdims=True
                )
                turned = pltpu.roll(jnp.broadcast_to(sums, (8, EDGE)), half, 1)[0:1]
                diagonal = total[:, :EDGE]
                diagonal = jnp.where((row == EDGE - 1) & (column < half), sums, diagonal)
                diagonal = jnp.where((row == EDGE - 2) & (column < half), turned, diagonal)
                packed[pl.ds(first[i, i], EDGE), :] = diagonal
                for j in range(i + 1, blocks):
                    packed[pl.ds(first[i, j], EDGE), :] = total[
                        :, (j - i) * EDGE : (j - i + 1) * EDGE
                    ]

    part = a_keep.shape[0]
    a_keep[...] = packed[pl.ds(x * part, part), :]
    a_send[...] = packed[pl.ds((1 - x) * part, part), :]
    b_keep[...] = packed[pl.ds((2 + y) * part, part), :]
    b_send[...] = packed[pl.ds((3 - y) * part, part), :]


def halve_kernel(which, keep_ref, got_ref, *refs):
    keep_out, send_out = refs[-2:]
    bit = which()
    part = keep_out.shape[0]
    mine, theirs = pl.ds(bit * part, part), pl.ds((1 - bit) * part, part)
    keep_out[...] = keep_ref[mine, :] + got_ref[mine, :]
    send_out[...] = keep_ref[theirs, :] + got_ref[theirs, :]


def line_split_kernel(length, a_keep, a_got, b_keep, b_got, *refs):
    outs = refs[-length:]
    z = z_pos()
    part = a_keep.shape[0] // length
    for d in range(length):
        rows = pl.ds((z ^ d) * part, part)
        outs[d][:part, :] = a_keep[rows, :] + a_got[rows, :]
        outs[d][part:, :] = b_keep[rows, :] + b_got[rows, :]


def line_sum_kernel(*refs):
    total = refs[0][...]
    for ref in refs[1:-1]:
        total = total + ref[...]
    refs[-1][...] = total


def line_join_kernel(length, *refs):
    z = z_pos()
    a_out, b_out = refs[-2:]
    part = a_out.shape[0] // length
    for d in range(length):
        rows = pl.ds((z ^ d) * part, part)
        a_out[rows, :] = refs[d][:part, :]
        b_out[rows, :] = refs[d][part:, :]


def pair_join_kernel(which, own_ref, got_ref, *refs):
    out_ref = refs[-1]
    bit = which()
    part = own_ref.shape[0]
    out_ref[pl.ds(bit * part, part), :] = own_ref[...]
    out_ref[pl.ds((1 - bit) * part, part), :] = got_ref[...]


def unpack_kernel(row_total, *refs):
    own_rows, average_out, *pairs, halves, centred = refs[-2 * CUTS - 4 :]
    own_pair, other_pair = pairs[:CUTS], pairs[CUTS:]
    core, x, y = core_bit(), x_bit(), y_bit()
    part = refs[0].shape[0]
    for h in range(2):
        base = 4 * part * h
        a_own, a_got, b_own, b_got = refs[4 * h : 4 * h + 4]
        halves[pl.ds(base + x * part, part), :] = a_own[...]
        halves[pl.ds(base + (1 - x) * part, part), :] = a_got[...]
        halves[pl.ds(base + (2 + y) * part, part), :] = b_own[...]
        halves[pl.ds(base + (3 - y) * part, part), :] = b_got[...]
    feat = own_rows.shape[1]
    blocks = feat // EDGE
    half_blocks = blocks // 2
    places = packed_places(blocks)
    row = lax.broadcasted_iota(jnp.int32, (EDGE, EDGE), 0)
    column = lax.broadcasted_iota(jnp.int32, (EDGE, EDGE), 1)
    lane = lax.broadcasted_iota(jnp.int32, (1, EDGE), 1)
    scale = 1.0 / row_total
    for side in range(2):

        @pl.when(core == side)
        def _():
            start = {}
            for owner in range(2):
                base = 0 if owner == side else 4 * part
                for i, j, first in places[owner]:
                    start[i, j] = base + first
            across, down = [], []
            for i in range(blocks):
                tail = halves[pl.ds(start[i, i] + EDGE - 8, 8), :]
                turned = pltpu.roll(tail, EDGE // 2, 1)
                average = jnp.where(lane < EDGE // 2, tail[7:8], turned[6:7]) * scale
                average_out[:, i * EDGE : (i + 1) * EDGE] = average
                wide = jnp.broadcast_to(average, (EDGE, EDGE))
                across.append(average)
                down.append(jnp.transpose(wide))
            squares = jnp.zeros((EDGE, EDGE), F32)

            def put(i, j, block):
                p, q = (i + half_blocks * side) % blocks, (j + half_blocks * side) % blocks
                centred[pl.ds(p * EDGE, EDGE), pl.ds(q * EDGE, EDGE)] = block

            for i in range(blocks):
                for j in range(i, blocks):
                    block = halves[pl.ds(start[i, j], EDGE), :] * scale - down[i] * across[j]
                    if i == j:
                        block = jnp.where(column >= row, block, jnp.transpose(block))
                        block = block + jnp.where(row == column, COV_EPS, 0.0)
                        squares = squares + block * block
                        put(i, i, block)
                    else:
                        squares = squares + 2.0 * (block * block)
                        put(i, j, block)
                        put(j, i, jnp.transpose(block))
            norm = jnp.sqrt(jnp.sum(jnp.sum(squares, axis=0, keepdims=True), axis=1, keepdims=True))
            factor = 1.0 / norm
            middle = feat // 2
            own = centred[:middle, :] * factor
            own_rows[...] = own
            split_into(own, own_pair)
            theirs = jnp.concatenate([centred[middle:, middle:], centred[middle:, :middle]], axis=1)
            split_into(theirs * factor, other_pair)


def two(value):
    high = value.astype(BF16)
    return high, (value - high.astype(F32)).astype(BF16)


def split_into(value, pair_refs):
    high, low = two(value)
    both = jnp.concatenate([high, low], axis=0)
    rows = both.shape[0] // len(pair_refs)
    for k, ref in enumerate(pair_refs):
        ref[...] = both[k * rows : (k + 1) * rows, :]


def load_full(own_refs, other_refs, high_ref, low_ref):
    middle = high_ref.shape[0] // 2
    rows = own_refs[0].shape[0]
    for k, (own_ref, other_ref) in enumerate(zip(own_refs, other_refs)):
        full = high_ref if k * rows < middle else low_ref
        first = k * rows % middle
        mine = pl.ds(first, rows)
        theirs = pl.ds(middle + first, rows)
        full[mine, :] = own_ref[...]
        full[theirs, :middle] = other_ref[:, middle:]
        full[theirs, middle:] = other_ref[:, :middle]


def times(high, low, high_ref, low_ref):
    return (
        jnp.dot(high, high_ref[...], preferred_element_type=F32)
        + jnp.dot(high, low_ref[...], preferred_element_type=F32)
        + jnp.dot(low, high_ref[...], preferred_element_type=F32)
    )


def power_kernel(exact, own_ref, *refs):
    pair, other = refs[:CUTS], refs[CUTS : 2 * CUTS]
    out_ref, *out_pair, high, low = refs[-CUTS - 3 :]
    load_full(pair, other, high, low)
    middle = own_ref.shape[0]
    square = times(high[:middle, :], low[:middle, :], high, low)
    if exact:
        cube = times(*two(square), high, low)
    else:
        cube = jnp.dot(square.astype(BF16), high[...], preferred_element_type=F32)
    result = 2.25 * own_ref[...] - 1.5 * square + 0.25 * cube
    out_ref[...] = result
    split_into(result, out_pair)


def root_kernel(factor, first, last, own_ref, root_ref, *refs):
    pair, other = refs[:CUTS], refs[CUTS : 2 * CUTS]
    out_ref, high, low = refs[-3:]
    load_full(pair, other, high, low)
    root = root_ref[...] * -0.5 if first else root_ref[...]
    if first:
        product = jnp.dot(root.astype(BF16), high[...], preferred_element_type=F32)
    else:
        product = times(*two(root), high, low)
    result = 1.5 * root - 0.5 * factor * own_ref[...] - 0.5 * product
    if last:
        row = lax.broadcasted_iota(jnp.int32, result.shape, 0)
        column = lax.broadcasted_iota(jnp.int32, result.shape, 1)
        result = (result + jnp.where(row == column, 1.5 * factor, 0.0)).astype(BF16)
    out_ref[...] = result


def whiten_rows(rows, root_ref, offset):
    projected = jnp.dot(rows, root_ref[...], preferred_element_type=F32) - offset
    energy = jnp.sum(projected * projected, axis=1, keepdims=True)
    return (projected * lax.rsqrt(energy + UNIT_EPS)).astype(BF16)


def build_root(own_root, other_root, average_ref, root, offset_ref):
    core = core_bit()
    middle, feat = own_root.shape
    root[pl.ds(core * middle, middle), :] = own_root[...]
    theirs = pl.ds((1 - core) * middle, middle)
    root[theirs, : feat // 2] = other_root[:, feat // 2 :]
    root[theirs, feat // 2 :] = other_root[:, : feat // 2]
    average = jnp.broadcast_to(average_ref[...], (16, feat))
    high, low = two(average)
    lowest = (average - high.astype(F32) - low.astype(F32)).astype(BF16)
    offset_ref[...] = (
        jnp.dot(high, root[...], preferred_element_type=F32)
        + jnp.dot(low, root[...], preferred_element_type=F32)
        + jnp.dot(lowest, root[...], preferred_element_type=F32)
    )[0:1]


def similarity(own_units, units):
    return lax.dot_general(
        own_units, units, (((1,), (1,)), ((), ())), preferred_element_type=F32
    )


def column_ids(ids):
    return jnp.transpose(jnp.broadcast_to(ids, (ids.shape[1], ids.shape[1])))


def off_diagonal(rows):
    row = lax.broadcasted_iota(jnp.int32, (rows, rows), 0)
    return row != lax.broadcasted_iota(jnp.int32, (rows, rows), 1)


def highest(best):
    return jnp.max(jnp.transpose(best), axis=0, keepdims=True)


def score_column_kernel(
    length, own_root, other_root, average_ref, ids_ref, values_ref, beside_ref, *refs
):
    column, (out_ref, beside_out, root, offset_ref) = refs[:-4], refs[-4:]
    me = lax.axis_index("grp")
    build_root(own_root, other_root, average_ref, root, offset_ref)
    offset = offset_ref[...]
    own = whiten_rows(values_ref[...], root, offset)
    beside = whiten_rows(beside_ref[...], root, offset)
    own_ids, beside_ids = column_ids(ids_ref[0:1, :]), column_ids(ids_ref[1:2, :])
    best = beside_best = None
    for t in range(length):
        units = whiten_rows(column[t - 1][...], root, offset) if t else own
        source = (z_pos() + t) % length * 2 + x_bit()
        ids = ids_ref[pl.ds(source ^ me, 1), :]
        same = own_ids == ids
        if t == 0:
            same = same & off_diagonal(values_ref.shape[0])
        found = jnp.where(same, similarity(own, units), -1.0)
        beside_found = jnp.where(beside_ids == ids, similarity(beside, units), -1.0)
        best = jnp.maximum(best, found) if t else found
        beside_best = jnp.maximum(beside_best, beside_found) if t else beside_found
    out_ref[...] = highest(best)
    beside_out[...] = highest(beside_best)


def larger_kernel(first_ref, second_ref, out_ref):
    out_ref[...] = jnp.maximum(first_ref[...], second_ref[...])


def score_kernel(
    own_root, other_root, average_ref, ids_ref, values_ref, piece_ref,
    out_ref, root, offset_ref, own_units, best,
):
    step = pl.program_id(0)
    me = lax.axis_index("grp")

    @pl.when(step == 0)
    def _():
        build_root(own_root, other_root, average_ref, root, offset_ref)
        own_units[...] = whiten_rows(values_ref[...], root, offset_ref[...])
        best[...] = jnp.full(best.shape, -1.0, F32)

    units = whiten_rows(piece_ref[...], root, offset_ref[...])
    same = column_ids(ids_ref[0:1, :]) == ids_ref[pl.ds(step ^ me, 1), :]
    same = same & (off_diagonal(values_ref.shape[0]) | (step != me))
    best[...] = jnp.maximum(best[...], jnp.where(same, similarity(own_units[...], units), -1.0))

    @pl.when(step == pl.num_programs(0) - 1)
    def _():
        out_ref[...] = highest(best[...])


def pick_kernel(limit, near_ref, far_ref, out_ref):
    z = z_pos()

    def put(ref):
        out_ref[...] = ref[...]

    pl.when(z < limit)(lambda: put(near_ref))
    pl.when(z >= limit)(lambda: put(far_ref))


def hold_kernel(source_ref, *refs):
    refs[-1][...] = source_ref[...]


def hold(array, after):
    return call(
        hold_kernel, [jax.ShapeDtypeStruct(array.shape, array.dtype)], [array], after=after
    )[0]


def join_kernel(first_ref, second_ref, out_ref):
    rows = first_ref.shape[0]
    out_ref[:rows, :] = first_ref[...]
    out_ref[rows:, :] = second_ref[...]


class Ids:
    def __init__(self, cluster):
        self.size = lax.axis_size("grp")
        self.held = cluster.reshape(1, cluster.shape[0])

    def step(self):
        count, columns = self.held.shape
        if count < self.size:
            got = swap(self.held, "grp", count)
            (self.held,) = call(
                join_kernel, [shape(2 * count, columns, jnp.int32)], [self.held, got]
            )
        return [self.held]

    def all(self):
        while self.held.shape[0] < self.size:
            self.step()
        return self.held


class Gather:
    def __init__(self, values):
        self.length = lax.axis_size("grp") // 2
        self.values = values
        self.right, self.left = {0: values}, {0: values}

    def along(self, t, after=()):
        size, length = 2 * self.length, self.length
        right, left = self.right[t - 1], self.left[t - 1]
        if after:
            right, left = hold(right, after), hold(left, after)
        to_left = [(g, g - 2) for g in range(size) if 1 <= g // 2 <= length - t]
        to_right = [(g, g + 2) for g in range(size) if t - 1 <= g // 2 <= length - 2]
        self.right[t] = lax.ppermute(right, "grp", to_left)
        self.left[t] = lax.ppermute(left, "grp", to_right)
        return [self.right[t], self.left[t]]

    def across(self, after=()):
        self.beside = swap(hold(self.values, after) if after else self.values, "grp", 1)
        return [self.beside]

    def column(self):
        pieces = []
        for t in range(1, self.length):
            kernel = functools.partial(pick_kernel, self.length - t)
            both = [self.right[t], self.left[self.length - t]]
            pieces += call(kernel, [shape(*self.values.shape, BF16)], both)
        return pieces


def best_cosines(own_root, other_root, average, ids, values, gathered):
    rows, feat = values.shape
    group = lax.axis_size("grp")
    scratch = [pltpu.VMEM((feat, feat), BF16), pltpu.VMEM((1, feat), F32)]
    flops = 2 * group * rows * feat * (feat + rows)
    ins = [own_root, other_root, average, ids, values]
    if isinstance(gathered, Gather):
        kernel = functools.partial(score_column_kernel, gathered.length)
        ins += [gathered.beside] + gathered.column()
        both = [shape(1, rows)] * 2
        best, beside = call(kernel, both, ins, flops, scratch, SCORE_BYTES)
        return call(larger_kernel, [shape(1, rows)], [best, swap(beside, "grp", 1)])[0]
    full = lambda array: pl.BlockSpec(array.shape, lambda i: (0, 0))
    return pl.pallas_call(
        score_kernel,
        grid=(group,),
        out_shape=shape(1, rows),
        in_specs=[full(array) for array in ins] + [pl.BlockSpec((rows, feat), lambda i: (i, 0))],
        out_specs=pl.BlockSpec((1, rows), lambda i: (0, 0)),
        scratch_shapes=scratch + [pltpu.VMEM((rows, feat), BF16), pltpu.VMEM((rows, rows), F32)],
        compiler_params=pltpu.CompilerParams(vmem_limit_bytes=SCORE_BYTES),
        cost_estimate=pl.CostEstimate(
            flops=flops, bytes_accessed=2 * group * rows * feat, transcendentals=0
        ),
    )(*ins, gathered)


def reduce_gram(values, blocks, gather, ids):
    length = lax.axis_size("grp") // 2
    part = -(-EDGE * (blocks * (blocks + 1) // 2) // (16 * length * 8)) * 8
    rows = part * length * 8
    swapped = swap(values, "rep", 1)
    a_keep, a_send, b_keep, b_send = call(
        gram_kernel,
        [shape(rows // 4, EDGE)] * 4,
        [values, swapped],
        flops=values.shape[0] * 2 * rows * EDGE * 2,
        scratch=[pltpu.VMEM((rows, EDGE), F32)],
    )
    a_got, b_got = swap(a_send, "grp", 1), swap(b_send, "rep", 2)
    second = [shape(rows // 8, EDGE)] * 2
    wait = ids.step()
    a_keep, a_send = call(functools.partial(halve_kernel, y_bit), second, [a_keep, a_got], after=wait)
    b_keep, b_send = call(functools.partial(halve_kernel, x_bit), second, [b_keep, b_got], after=wait)
    wait = ids.step()
    a_got, b_got = swap(a_send, "rep", 2), swap(b_send, "grp", 1)
    pieces = call(
        functools.partial(line_split_kernel, length),
        [shape(2 * part, EDGE)] * length,
        [a_keep, a_got, b_keep, b_got],
        after=wait + (gather.along(1) if gather else []),
    )
    got = [swap(pieces[d], "grp", 2 * d) for d in range(1, length)]
    (total,) = call(line_sum_kernel, [shape(2 * part, EDGE)], [pieces[0]] + got)
    got = [swap(total, "grp", 2 * d) for d in range(1, length)]
    wait = gather.across([pieces[0]]) if gather else []
    a_own, b_own = call(
        functools.partial(line_join_kernel, length), second, [total] + got, after=wait
    )
    wait = gather.along(2, [a_own]) if gather else []
    a_got, b_got = swap(a_own, "rep", 2), swap(b_own, "grp", 1)
    third = [shape(rows // 4, EDGE)]
    late = ids.step()
    (a_own,) = call(functools.partial(pair_join_kernel, y_bit), third, [a_own, a_got], after=late)
    (b_own,) = call(functools.partial(pair_join_kernel, x_bit), third, [b_own, b_got], after=late)
    a_got, b_got = swap(a_own, "grp", 1), swap(b_own, "rep", 2)
    own = [a_own, a_got, b_own, b_got]
    return own + [swap(piece, "rep", 1) for piece in own], wait


def inverse_root_slabs(own, pair, other, feat, gather, after):
    middle = feat // 2
    full = [pltpu.VMEM((feat, feat), BF16)] * 2
    flops = 2 * 3 * middle * feat * feat
    outs = [shape(middle, feat)] + [shape(2 * middle // CUTS, feat, BF16)] * CUTS
    root, factor = own, 1.5
    waits = {4: gather.along(3, [own])} if gather else {}
    for step in range(STEPS):
        last = step == STEPS - 1
        if not last:
            power, *power_pair = call(
                functools.partial(power_kernel, step >= EXACT_FROM), outs, [own] + pair + other, 2 * flops, full, NEWTON_BYTES, after if step else ()
            )
            power_other = [swap(piece, "rep", 1) for piece in power_pair]
        if step > 0:
            (root,) = call(
                functools.partial(root_kernel, factor, step == 1, last),
                [shape(middle, feat, BF16 if last else F32)],
                [own, root] + pair + other,
                flops,
                full,
                NEWTON_BYTES,
                waits.get(step, ()),
            )
            factor, after = 1.5 * factor, [root]
        if not last:
            own, pair, other = power, power_pair, power_other
    return root, swap(root, "rep", 1)


def local(embeddings, scales, cluster, cluster_rank):
    row_count, feat = embeddings.shape
    group = lax.axis_size("grp")
    row_total = row_count * group * lax.axis_size("rep")
    (values,) = call(dequantize_kernel, [shape(row_count, feat, BF16)], [embeddings, scales])
    ids = Ids(cluster)
    gather, gathered = None, None
    if group * values.size * values.dtype.itemsize <= IN_PIECES_BYTES:
        gather = Gather(values)
    else:
        gathered = lax.all_gather(values, "grp", axis=0, tiled=True)
    pieces, wait = reduce_gram(values, feat // EDGE, gather, ids)
    middle = feat // 2
    pair_shapes = [shape(2 * middle // CUTS, feat, BF16)] * (2 * CUTS)
    own, average, *pairs = call(
        functools.partial(unpack_kernel, row_total),
        [shape(middle, feat), shape(1, feat)] + pair_shapes,
        pieces,
        scratch=[pltpu.VMEM((8 * pieces[0].shape[0], EDGE), F32), pltpu.VMEM((feat, feat), F32)],
        limit=UNPACK_BYTES,
    )
    own_root, other_root = inverse_root_slabs(own, pairs[:CUTS], pairs[CUTS:], feat, gather, wait)
    best = best_cosines(own_root, other_root, average, ids.all(), values, gather or gathered)
    return best.reshape(row_count)


def solution(mesh):
    placed = (
        P(("grp", "rep"), None),
        P(("grp", "rep"), None),
        P(("grp", "rep")),
        P(("grp", "rep")),
    )
    return jax.shard_map(
        local, mesh=mesh, in_specs=placed, out_specs=P(("grp", "rep")), check_vma=False
    )
```
